512 devices in a mesh: blk: 256 (over y_lo, z, x, core), head: 2 (over y_hi).
Axes of the slice: x: 4, y: 4 (y_hi: 2, y_lo: 2; y = y_hi * 2 + y_lo), z: 16, core: 2. Of those that a mesh axis runs over, the one named last changes fastest.
Arguments:
- block_table: int32 [256, 2], P('blk'), may hold values from 0 to 511, as said below
- a_query: bfloat16 [6, 32, 98304], P(None, 'head', 'blk'), may hold values from -8 to 8
- b_query: bfloat16 [98304, 768], P(('blk', 'head')), may hold values from -60 to 60
- a_key: bfloat16 [2, 32, 98304], P(None, 'head', 'blk'), may hold values from -8 to 8
- b_key: bfloat16 [98304, 256], P(('blk', 'head')), may hold values from -6 to 6
- a_value: bfloat16 [2, 32, 98304], P(None, 'head', 'blk'), may hold values from -6 to 6
- b_value: bfloat16 [98304, 256], P(('blk', 'head')), may hold values from -6 to 6
Outputs:
- attended: bfloat16 [32, 98304, 128], P('head', 'blk')
- log_total: float32 [32, 98304], P('head', 'blk')
The draws below stay inside these ranges and needn't reach their ends.
Inputs may be any that keep to these rules, and one draw needn't show every extreme that they name: `block_table`: row e holds a block b below 256 and the block 511 - b; every block of the sequence appears exactly once.
All inputs are finite; a program needn't handle non-finite values.
Results may differ from the reference program's by a relative error of at most 0.012.
The reference program's roundings to bfloat16 on the way count: a program that leaves them out, or rounds other values in their place, can miss the bound.
Values may be sent and summed in bfloat16 or wider, within the bound.
A program may use at most 64 MiB of HBM per device.

```python
import math
import jax
import jax.numpy as jnp
from jax import lax

H = 32
DH = 128
RQ = 6
RK = 2
HALF = 192
STEPS = 4
PLACES = 256
SEQ = 98304


def draw_block_table(key, part):
    key = jax.random.fold_in(key, 11)
    order = jax.random.permutation(key, PLACES).astype(jnp.int32)
    return jnp.stack([order, 2 * PLACES - 1 - order], axis=1).astype(jnp.int32)


def draw_b_query(key, part):
    key = jax.random.fold_in(key, 23)
    first_key = jax.random.fold_in(key, 0)
    values = jax.random.normal(first_key, (SEQ, RQ * DH), jnp.float32)
    return jnp.clip(values, -6.0, 6.0).astype(jnp.bfloat16)


def block_levels(stream_key, extent, shards, least, top_value):
    level, own = 1.0, jax.random.fold_in(stream_key, 6)
    for axis_at, blocks in shards:
        heights = jnp.exp(jax.random.uniform(jax.random.fold_in(own, axis_at), (blocks,), jnp.float32, least / len(shards), top_value / len(shards)))
        level = level * jnp.repeat(heights, extent[axis_at] // blocks).reshape([-1 if axis == axis_at else 1 for axis in range(len(extent))])
    return level


def scatter_about(stream_key, shape, deviation, most, pieces=(), kind=jnp.bfloat16):
    result = jax.random.normal(stream_key, shape, jnp.float32) * deviation
    if len(pieces) > 0:
        result = block_levels(stream_key, shape, pieces, -0.22, 0.18) * result
    return jnp.clip(result, min=-most, max=most).astype(kind)


def setup_inputs(seed: int = 0) -> dict:
    streams_of = jax.random.split(jax.random.key(seed), 8)
    block_table = draw_block_table(jax.random.fold_in(streams_of[7], 71), 0)
    a_query = scatter_about(streams_of[1], (RQ, H, SEQ), 1.5, 8.0, ((1, 2), (2, 256)))
    b_query = draw_b_query(jax.random.fold_in(streams_of[7], 71), 0)
    a_key = scatter_about(streams_of[3], (RK, H, SEQ), 1.5, 8.0, ((1, 2), (2, 256)))
    b_key = scatter_about(streams_of[4], (SEQ, RK * DH), 1.0, 6.0, ((0, 512),))
    a_value = scatter_about(streams_of[5], (RK, H, SEQ), 1.0, 6.0, ((1, 2), (2, 256)))
    b_value = scatter_about(streams_of[6], (SEQ, RK * DH), 1.0, 6.0, ((0, 512),))
    return {"block_table": block_table, "a_query": a_query, "b_query": b_query, "a_key": a_key, "b_key": b_key, "a_value": a_value, "b_value": b_value}


masked_fill = -1e+30

def build_heads(factor_a, factor_b, rank_size):
    row_total = factor_b.shape[0]
    blocked = factor_b.reshape(row_total, rank_size, -1).astype(jnp.float32)
    product = jnp.einsum('rht,trd->htd', factor_a.astype(jnp.float32), blocked)
    return (product * (1.0 / rank_size)).astype(jnp.bfloat16)

def reference(block_table, a_query, b_query, a_key, b_key, a_value, b_value):
    row_count = 2 * HALF
    offsets = jnp.arange(HALF, dtype=jnp.int32)
    score_scale = 1.0 / math.sqrt(DH)

    def positions(device):
        block_pair = lax.dynamic_slice_in_dim(block_table, device, 1, 0)[0]
        return (block_pair[:, None] * HALF + offsets[None, :]).reshape(row_count)

    def factors(array_a, array_b, device):
        first_row = (device * row_count).astype(jnp.int32)
        return (lax.dynamic_slice_in_dim(array_a, first_row, row_count, 2), lax.dynamic_slice_in_dim(array_b, first_row, row_count, 0))

    def one_device(device):
        queries = build_heads(*factors(a_query, b_query, device), RQ)
        key_list = []
        value_list = []
        place_list = []
        for offset in range(STEPS):
            source = ((device - offset) % PLACES).astype(jnp.int32)
            key_list.append(build_heads(*factors(a_key, b_key, source), RK))
            value_list.append(build_heads(*factors(a_value, b_value, source), RK))
            place_list.append(positions(source))
        key_heads = jnp.concatenate(key_list, axis=1)
        value_heads = jnp.concatenate(value_list, axis=1)
        key_places = jnp.concatenate(place_list, axis=0)
        query_places = positions(device)
        scores = jnp.einsum('hqd,hkd->hqk', queries.astype(jnp.float32), key_heads.astype(jnp.float32)) * score_scale
        visible = (key_places[None, :] <= query_places[:, None])[None]
        running_max = lax.optimization_barrier(jnp.max(jnp.where(visible, scores, masked_fill), axis=2))
        weights = jnp.where(visible, jnp.exp(scores - running_max[..., None]), 0.0)
        running_sum = lax.optimization_barrier(jnp.sum(weights, axis=2))
        rounded = weights.astype(jnp.bfloat16)
        mixed = jnp.einsum('hqk,hkd->hqd', rounded.astype(jnp.float32), value_heads.astype(jnp.float32))
        mixed = mixed / running_sum[..., None]
        return (mixed.astype(jnp.bfloat16), running_max + jnp.log(running_sum))
    devices = jnp.arange(PLACES, dtype=jnp.int32)
    outputs, logs = lax.map(one_device, devices)
    attended = jnp.transpose(outputs, (1, 0, 2, 3)).reshape(H, SEQ, DH)
    log_total = jnp.transpose(logs, (1, 0, 2)).reshape(H, SEQ)
    return (attended, log_total)
```

```python
import math

import jax
import jax.numpy as jnp
from jax import lax
from jax.experimental import pallas as pl
from jax.experimental.pallas import tpu as pltpu
from jax.sharding import PartitionSpec as P

HALF = 192
DH = 128
PAIRS = 8
RQ = 6
MESH = pl.DeviceIdType.MESH
F32 = jnp.float32
BF16 = jnp.bfloat16
SCALE = 0.5 / math.sqrt(DH)
SCALE2 = SCALE * math.log2(math.e)
MASKED = -1e30


def kernel(
    bt_in, aq_in, bq_in, ak_in, bk_in, av_in, bv_in,
    out_ref, log_ref,
    bt, bts, aq, bq, bkv, akv,
    bqt, a2q, qbd, bkf, bvt, akt, avj,
    o_own, m_own, l_own, o_acc, m_acc, l_acc, logs,
    local_sem, bts_sem, ex_send, ex_recv, a_send, a_recv, f_send, f_recv, t_send, t_recv, b_send, b_recv,
):
    e = lax.axis_index("blk")
    h = lax.axis_index("head")
    places = lax.axis_size("blk")
    other = 1 - h
    core = lax.rem(e, 2)
    lane = lax.broadcasted_iota(jnp.int32, (1, 2 * HALF), 1)
    first = lane < HALF

    def at(blk, head):
        return {"blk": lax.rem(blk + places, places), "head": head}

    barrier = pltpu.get_barrier_semaphore()
    pl.semaphore_signal(barrier, inc=1, device_id=at(e - 1, h), device_id_type=MESH)
    pl.semaphore_signal(barrier, inc=1, device_id=at(e, other), device_id_type=MESH)

    @pl.when(core == 0)
    def _():
        pl.semaphore_signal(barrier, inc=1, device_id=at(e - 2, h), device_id_type=MESH)

    locals_ = [
        pltpu.make_async_copy(src, dst, local_sem.at[i])
        for i, (src, dst) in enumerate(
            [
                (bk_in, bkv.at[0, h, 0]),
                (bv_in, bkv.at[0, h, 1]),
                (ak_in, akv.at[0, pl.ds(0, 2)]),
                (av_in, akv.at[0, pl.ds(2, 2)]),
                (bq_in, bq.at[h]),
                (aq_in, aq),
            ]
        )
    ]
    for copy in locals_:
        copy.start()
    own0, own1 = bt_in[0, 0], bt_in[0, 1]
    tlane = lax.broadcasted_iota(jnp.int32, (8, 128), 1)
    bt[0] = jnp.where(tlane == 0, own0, own1)

    @pl.when(core == 0)
    def _():
        pl.semaphore_wait(barrier, 3)

    @pl.when(core == 1)
    def _():
        pl.semaphore_wait(barrier, 2)

    def remote(src, dst, send, recv, target):
        return pltpu.make_async_remote_copy(
            src_ref=src, dst_ref=dst, send_sem=send, recv_sem=recv, device_id=target, device_id_type=MESH
        )

    def half_copy(slot, half, s_from, s_to, target):
        sems = (a_send, a_recv) if half is h else (b_send, b_recv)
        return remote(
            bkv.at[s_from, half], bkv.at[s_to, half], sems[0].at[slot], sems[1].at[s_to - 1], target
        )

    def a_copies(slot, s_from, s_to, target):
        return [
            half_copy(slot, h, s_from, s_to, target),
            remote(akv.at[s_from], akv.at[s_to], f_send.at[slot], f_recv.at[s_to - 1], target),
            remote(bt.at[s_from], bt.at[s_to], t_send.at[slot], t_recv.at[s_to - 1], target),
        ]

    def b_copies(slot, s_from, s_to, target):
        return [half_copy(slot, other, s_from, s_to, target)]

    near, far = at(e + 1, h), at(e + 2, h)
    partner = at(e, other)

    def start(copies):
        for copy in copies:
            copy.start()

    def first_sends(copies):
        start(copies(0, 0, 1, near))

    def forward_one(copies):
        @pl.when(core == 0)
        def _():
            start(copies(1, 1, 2, near))
            start(copies(2, 0, 2, far))
            start(copies(3, 1, 3, far))

    def forward_two(copies):
        @pl.when(core == 0)
        def _():
            start(copies(4, 2, 3, near))

    def wait_a(s):
        for copy in a_copies(0, s - 1, s, near):
            copy.wait_recv()

    def wait_b(s):
        for copy in b_copies(0, s - 1, s, near):
            copy.wait_recv()

    ex_kv = remote(bkv.at[0, h], bkv.at[0, h], ex_send.at[0], ex_recv.at[0], partner)
    ex_q = remote(bq.at[h], bq.at[h], ex_send.at[1], ex_recv.at[1], partner)
    for copy in locals_[:4]:
        copy.wait()
    ex_kv.start()
    first_sends(a_copies)
    locals_[4].wait()
    ex_q.start()
    locals_[5].wait()

    def scalars(s):
        copy = pltpu.make_async_copy(bt.at[s], bts.at[s], bts_sem.at[s])
        copy.start()
        copy.wait()
        b0, b1 = bts[s, 0, 0], bts[s, 0, 1]
        return (b0 > b1).astype(jnp.int32), jnp.minimum(b0, b1)

    def prep_a(s):
        x = akv[s].astype(F32)
        keys = x[0:2].reshape(32, 2 * HALF)
        keys_t = jnp.concatenate([keys, jnp.zeros((96, 2 * HALF), F32)], axis=0).T
        akt[s, 0] = keys_t[:HALF]
        akt[s, 1] = keys_t[HALF:]
        avj[s, 0] = x[2:4, :, :HALF]
        avj[s, 1] = x[2:4, :, HALF:]

    def prep_b(s, j):
        bkf[s, j] = bkv[s, j, 0].astype(F32)
        v = bkv[s, j, 1].astype(F32)
        v = jnp.concatenate([v, jnp.zeros((64, 2 * DH), F32)], axis=0).T
        bvt[s, j] = v[:, :HALF]

    def prep_q(j):
        b = bq[j].astype(F32)
        bqt[j] = jnp.concatenate([b, b], axis=0).T.astype(BF16)

    def prep_aq():
        x = aq[...].astype(F32)
        low, high = x[:, :PAIRS], x[:, PAIRS:]
        wide = first[None]

        def turned(y):
            return pltpu.roll(y.reshape(RQ * PAIRS, 2 * HALF), HALF, 1).reshape(y.shape)

        a2q[0] = jnp.where(wide, low, turned(high))
        a2q[1] = jnp.where(wide, turned(low), high)

    def build_q(j, p):
        total = a2q[j, 0, pl.ds(p, 1), :] * bqt[j, 0:DH, :].astype(F32)
        for r in range(1, RQ):
            total += a2q[j, r, pl.ds(p, 1), :] * bqt[j, r * DH : (r + 1) * DH, :].astype(F32)
        total = total * (1.0 / RQ)
        qbd[j, p, 0:DH] = jnp.where(first, total, 0.0).astype(BF16)
        qbd[j, p, DH : 2 * DH] = jnp.where(first, 0.0, total).astype(BF16)

    def build_kv(s, j, p):
        a = pltpu.roll(akt[s, j], lax.rem(128 - p, 128), 1)
        b0, b1 = bkf[s, j, :, 0:DH], bkf[s, j, :, DH : 2 * DH]
        ka = a[:, 0:1] * b0 + a[:, 16:17] * b1
        kb = a[:, 8:9] * b0 + a[:, 24:25] * b1
        keys = jnp.concatenate([ka.astype(BF16), kb.astype(BF16)], axis=1)
        c0, c1 = bvt[s, j, 0:DH], bvt[s, j, DH : 2 * DH]
        va = avj[s, j, 0, pl.ds(p, 1), :] * c0 + avj[s, j, 1, pl.ds(p, 1), :] * c1
        vb = avj[s, j, 0, pl.ds(p + PAIRS, 1), :] * c0 + avj[s, j, 1, pl.ds(p + PAIRS, 1), :] * c1
        values = jnp.concatenate([va.astype(BF16), vb.astype(BF16)], axis=0)
        return keys, values

    def dot(x, y):
        return jnp.dot(x, y, preferred_element_type=F32)

    def weigh(scores, top, values):
        weights = jnp.exp2((scores - top) * SCALE2)
        total = jnp.sum(weights, axis=0, keepdims=True)
        both = dot(values, weights.astype(BF16))
        return total, jnp.where(first, both[:DH], both[DH:])

    def highest(scores):
        return jnp.max(scores, axis=0, keepdims=True)

    def merge(state, scores, values):
        m, l, o = state
        top = jnp.maximum(m, highest(scores))
        total, added = weigh(scores, top, values)
        rescale = jnp.exp2((m - top) * SCALE2)
        return top, l * rescale + total, o * rescale + added

    def diagonal(j, p):
        keys, values = build_kv(0, j, p)
        scores = dot(keys, qbd[j, p])
        row = lax.broadcasted_iota(jnp.int32, scores.shape, 0)
        col = lax.broadcasted_iota(jnp.int32, scores.shape, 1)
        col = jnp.where(col < HALF, col, col - HALF)
        scores = jnp.where(row <= col, scores, MASKED)
        top = highest(scores)
        total, added = weigh(scores, top, values)
        m_own[j, p] = top
        l_own[j, p] = total
        o_own[j, p] = added

    def each_pair(body):
        def step(p, carry):
            body(p)
            return carry

        lax.fori_loop(0, PAIRS, step, 0)

    jl0, low0 = scalars(0)
    prep_aq()
    prep_a(0)
    prep_q(h)
    prep_b(0, h)

    def own_half(p):
        build_q(h, p)
        diagonal(h, p)

    each_pair(own_half)

    ex_kv.wait_recv()
    first_sends(b_copies)
    wait_a(1)
    forward_one(a_copies)
    prep_b(0, other)
    ex_q.wait_recv()
    prep_q(other)

    def other_half(p):
        build_q(other, p)
        diagonal(other, p)

    each_pair(other_half)
    wait_b(1)
    forward_one(b_copies)

    def low_keys(p):
        keys, values = build_kv(0, jl0, p)
        scores = dot(keys, qbd[1 - jl0, p])
        m, l, o = merge((m_own[1 - jl0, p], l_own[1 - jl0, p], o_own[1 - jl0, p]), scores, values)
        m_acc[1, p], l_acc[1, p], o_acc[1, p] = m, l, o
        m_acc[0, p], l_acc[0, p], o_acc[0, p] = m_own[jl0, p], l_own[jl0, p], o_own[jl0, p]

    each_pair(low_keys)

    for s in range(1, 4):
        if s > 1:
            wait_a(s)
            if s == 2:
                forward_two(a_copies)
            wait_b(s)
            if s == 2:
                forward_two(b_copies)
        jls, lows = scalars(s)
        pick = (lows > low0).astype(jnp.int32)
        jq = jl0 + pick - 2 * jl0 * pick
        jk = jls + pick - 2 * jls * pick
        prep_a(s)
        prep_b(s, 0)
        prep_b(s, 1)

        def one_offset(p):
            keys, values = build_kv(s, jls, p)
            scores = dot(keys, qbd[1 - jl0, p])
            keys2, values2 = build_kv(s, jk, p)
            scores2 = dot(keys2, qbd[jq, p])
            high = merge((m_acc[1, p], l_acc[1, p], o_acc[1, p]), scores, values)
            low = (m_acc[0, p], l_acc[0, p], o_acc[0, p])
            is_high = pick == 1
            old = tuple(jnp.where(is_high, x, y) for x, y in zip(high, low))
            new = merge(old, scores2, values2)
            m_acc[1, p], l_acc[1, p], o_acc[1, p] = (jnp.where(is_high, x, y) for x, y in zip(new, high))
            m_acc[0, p], l_acc[0, p], o_acc[0, p] = (jnp.where(is_high, x, y) for x, y in zip(low, new))

        each_pair(one_offset)

    def finish(p):
        for j in range(2):
            k = jl0 if j == 0 else 1 - jl0
            m, l, o = m_acc[k, p], l_acc[k, p], o_acc[k, p]
            rows = (o * (0.5 / l)).T.astype(BF16)
            out_ref[p, j * HALF : (j + 1) * HALF, :] = rows[:HALF]
            out_ref[p + PAIRS, j * HALF : (j + 1) * HALF, :] = rows[HALF:]
            logs[j, pl.ds(p, 1), :] = m * SCALE + jnp.log(l)

    each_pair(finish)
    log0, log1 = logs[0], logs[1]
    log_ref[0:PAIRS] = jnp.where(first, log0, pltpu.roll(log1, HALF, 1))
    log_ref[PAIRS:] = jnp.where(first, pltpu.roll(log0, HALF, 1), log1)

    ex_kv.wait_send()
    ex_q.wait_send()
    for copies in (a_copies, b_copies):
        for copy in copies(0, 0, 1, near):
            copy.wait_send()

    @pl.when(core == 0)
    def _():
        for copies in (a_copies, b_copies):
            for slot in range(1, 5):
                for copy in copies(slot, 0, 1, near):
                    copy.wait_send()


def on_device(block_table, a_query, b_query, a_key, b_key, a_value, b_value):
    rows = 2 * HALF
    heads = 2 * PAIRS
    hbm = pl.BlockSpec(memory_space=pl.ANY)
    vmem = pl.BlockSpec(memory_space=pltpu.VMEM)
    dma = pltpu.SemaphoreType.DMA
    return pl.pallas_call(
        kernel,
        out_shape=(
            jax.ShapeDtypeStruct((heads, rows, DH), BF16),
            jax.ShapeDtypeStruct((heads, rows), F32),
        ),
        in_specs=[pl.BlockSpec(memory_space=pltpu.SMEM)] + [hbm] * 6,
        out_specs=(vmem, vmem),
        scratch_shapes=[
            pltpu.VMEM((4, 8, 128), jnp.int32),
            pltpu.SMEM((4, 8, 128), jnp.int32),
            pltpu.VMEM((RQ, heads, rows), BF16),
            pltpu.VMEM((2, HALF, RQ * DH), BF16),
            pltpu.VMEM((4, 2, 2, HALF, 2 * DH), BF16),
            pltpu.VMEM((4, 4, heads, rows), BF16),
            pltpu.VMEM((2, RQ * DH, rows), BF16),
            pltpu.VMEM((2, RQ, PAIRS, rows), F32),
            pltpu.VMEM((2, PAIRS, 2 * DH, rows), BF16),
            pltpu.VMEM((4, 2, HALF, 2 * DH), F32),
            pltpu.VMEM((4, 2, 2 * DH, HALF), F32),
            pltpu.VMEM((4, 2, HALF, 128), F32),
            pltpu.VMEM((4, 2, 2, heads, HALF), F32),
            pltpu.VMEM((2, PAIRS, DH, rows), F32),
            pltpu.VMEM((2, PAIRS, 1, rows), F32),
            pltpu.VMEM((2, PAIRS, 1, rows), F32),
            pltpu.VMEM((2, PAIRS, DH, rows), F32),
            pltpu.VMEM((2, PAIRS, 1, rows), F32),
            pltpu.VMEM((2, PAIRS, 1, rows), F32),
            pltpu.VMEM((2, PAIRS, rows), F32),
            dma((6,)),
            dma((4,)),
            dma((2,)),
            dma((2,)),
            dma((5,)),
            dma((3,)),
            dma((5,)),
            dma((3,)),
            dma((5,)),
            dma((3,)),
            dma((5,)),
            dma((3,)),
        ],
        compiler_params=pltpu.CompilerParams(
            collective_id=0, has_side_effects=True, vmem_limit_bytes=48 * 1024 * 1024
        ),
    )(block_table, a_query, b_query, a_key, b_key, a_value, b_value)


def solution(mesh):
    in_specs = (
        P("blk", None),
        P(None, "head", "blk"),
        P(("blk", "head"), None),
        P(None, "head", "blk"),
        P(("blk", "head"), None),
        P(None, "head", "blk"),
        P(("blk", "head"), None),
    )
    out_specs = (P("head", "blk", None), P("head", "blk"))
    return jax.shard_map(
        on_device, mesh=mesh, in_specs=in_specs, out_specs=out_specs, check_vma=False
    )
```

```python
import math

import jax
import jax.numpy as jnp
from jax import lax
from jax.experimental import pallas as pl
from jax.experimental.pallas import tpu as pltpu
from jax.sharding import PartitionSpec as P

HALF = 192
DH = 128
PAIRS = 8
RQ = 6
MESH = pl.DeviceIdType.MESH
F32 = jnp.float32
BF16 = jnp.bfloat16
SCALE = 0.5 / math.sqrt(DH)
MASKED = -1e30


def kernel(
    bt_in, aq_in, bq_in, ak_in, bk_in, av_in, bv_in,
    out_hbm, log_hbm,
    out_ref, log_ref, bt, bts, aq, bq, bkv, akv,
    bqt, a2q, qbd, bkf, bvt, akt, avj, kb, vb,
    o_acc, m_acc, l_acc, logs,
    out_sem, local_sem, bts_sem, ex_send, ex_recv, a_send, a_recv, f_send, f_recv, t_send, t_recv, b_send, b_recv,
):
    e = lax.axis_index("blk")
    h = lax.axis_index("head")
    places = lax.axis_size("blk")
    other = 1 - h
    core = lax.rem(e, 2)
    lane = lax.broadcasted_iota(jnp.int32, (1, 2 * HALF), 1)
    first = lane < HALF

    def at(blk, head):
        return {"blk": lax.rem(blk + places, places), "head": head}

    barrier = pltpu.get_barrier_semaphore()
    pl.semaphore_signal(barrier, inc=1, device_id=at(e - 1, h), device_id_type=MESH)
    pl.semaphore_signal(barrier, inc=1, device_id=at(e, other), device_id_type=MESH)

    @pl.when(core == 0)
    def _():
        pl.semaphore_signal(barrier, inc=1, device_id=at(e - 2, h), device_id_type=MESH)

    locals_ = [
        pltpu.make_async_copy(src, dst, local_sem.at[i])
        for i, (src, dst) in enumerate(
            [
                (bk_in, bkv.at[0, h, 0]),
                (bv_in, bkv.at[0, h, 1]),
                (ak_in, akv.at[0, pl.ds(0, 2)]),
                (av_in, akv.at[0, pl.ds(2, 2)]),
                (bq_in, bq.at[h]),
                (aq_in, aq),
            ]
        )
    ]
    for copy in locals_:
        copy.start()
    own0, own1 = bt_in[0, 0], bt_in[0, 1]
    tlane = lax.broadcasted_iota(jnp.int32, (8, 128), 1)
    bt[0] = jnp.where(tlane == 0, own0, own1)

    @pl.when(core == 0)
    def _():
        pl.semaphore_wait(barrier, 3)

    @pl.when(core == 1)
    def _():
        pl.semaphore_wait(barrier, 2)

    def remote(src, dst, send, recv, target):
        return pltpu.make_async_remote_copy(
            src_ref=src, dst_ref=dst, send_sem=send, recv_sem=recv, device_id=target, device_id_type=MESH
        )

    def half_copy(slot, half, s_from, s_to, target):
        sems = (a_send, a_recv) if half is h else (b_send, b_recv)
        return remote(
            bkv.at[s_from, half], bkv.at[s_to, half], sems[0].at[slot], sems[1].at[s_to - 1], target
        )

    def a_copies(slot, s_from, s_to, target):
        return [
            half_copy(slot, h, s_from, s_to, target),
            remote(akv.at[s_from], akv.at[s_to], f_send.at[slot], f_recv.at[s_to - 1], target),
            remote(bt.at[s_from], bt.at[s_to], t_send.at[slot], t_recv.at[s_to - 1], target),
        ]

    def b_copies(slot, s_from, s_to, target):
        return [half_copy(slot, other, s_from, s_to, target)]

    near, far = at(e + 1, h), at(e + 2, h)
    partner = at(e, other)

    def start(copies):
        for copy in copies:
            copy.start()

    def first_sends(copies):
        start(copies(0, 0, 1, near))

    def forward_one(copies):
        @pl.when(core == 0)
        def _():
            start(copies(1, 1, 2, near))
            start(copies(2, 0, 2, far))
            start(copies(3, 1, 3, far))

    def forward_two(copies):
        @pl.when(core == 0)
        def _():
            start(copies(4, 2, 3, near))

    def wait_a(s):
        for copy in a_copies(0, s - 1, s, near):
            copy.wait_recv()

    def wait_b(s):
        for copy in b_copies(0, s - 1, s, near):
            copy.wait_recv()

    ex_kv = remote(bkv.at[0, h], bkv.at[0, h], ex_send.at[0], ex_recv.at[0], partner)
    ex_q = remote(bq.at[h], bq.at[h], ex_send.at[1], ex_recv.at[1], partner)
    for copy in locals_[:4]:
        copy.wait()
    ex_kv.start()
    first_sends(a_copies)
    locals_[4].wait()
    ex_q.start()
    locals_[5].wait()

    def scalars(s):
        copy = pltpu.make_async_copy(bt.at[s], bts.at[s], bts_sem.at[s])
        copy.start()
        copy.wait()
        b0, b1 = bts[s, 0, 0], bts[s, 0, 1]
        return (b0 > b1).astype(jnp.int32), jnp.minimum(b0, b1)

    def prep_a(s):
        x = akv[s].astype(F32)
        keys = x[0:2].reshape(32, 2 * HALF)
        keys_t = jnp.concatenate([keys, jnp.zeros((96, 2 * HALF), F32)], axis=0).T
        akt[s, 0] = keys_t[:HALF]
        akt[s, 1] = keys_t[HALF:]
        avj[s, 0] = x[2:4, :, :HALF]
        avj[s, 1] = x[2:4, :, HALF:]

    def prep_b(s, j):
        bkf[s, j] = bkv[s, j, 0].astype(F32)
        v = bkv[s, j, 1].astype(F32)
        v = jnp.concatenate([v, jnp.zeros((64, 2 * DH), F32)], axis=0).T
        bvt[s, j] = v[:, :HALF]

    def prep_q(j):
        b = bq[j].astype(F32)
        bqt[j] = jnp.concatenate([b, b], axis=0).T.astype(BF16)

    def prep_aq():
        x = aq[...].astype(F32)
        low, high = x[:, :PAIRS], x[:, PAIRS:]
        wide = first[None]

        def turned(y):
            return pltpu.roll(y.reshape(RQ * PAIRS, 2 * HALF), HALF, 1).reshape(y.shape)

        a2q[0] = jnp.where(wide, low, turned(high))
        a2q[1] = jnp.where(wide, turned(low), high)

    def build_q(j, p):
        total = a2q[j, 0, pl.ds(p, 1), :] * bqt[j, 0:DH, :].astype(F32)
        for r in range(1, RQ):
            total += a2q[j, r, pl.ds(p, 1), :] * bqt[j, r * DH : (r + 1) * DH, :].astype(F32)
        total = total * (1.0 / RQ)
        qbd[j, p, 0:DH] = jnp.where(first, total, 0.0).astype(BF16)
        qbd[j, p, DH : 2 * DH] = jnp.where(first, 0.0, total).astype(BF16)

    def build_kv(s, j, p):
        a = pltpu.roll(akt[s, j], lax.rem(128 - p, 128), 1)
        b0, b1 = bkf[s, j, :, 0:DH], bkf[s, j, :, DH : 2 * DH]
        ka = a[:, 0:1] * b0 + a[:, 16:17] * b1
        kb_ = a[:, 8:9] * b0 + a[:, 24:25] * b1
        c0, c1 = bvt[s, j, 0:DH], bvt[s, j, DH : 2 * DH]
        va = avj[s, j, 0, pl.ds(p, 1), :] * c0 + avj[s, j, 1, pl.ds(p, 1), :] * c1
        vb_ = avj[s, j, 0, pl.ds(p + PAIRS, 1), :] * c0 + avj[s, j, 1, pl.ds(p + PAIRS, 1), :] * c1
        kb[s, j, p, :, 0:DH] = ka.astype(BF16)
        kb[s, j, p, :, DH : 2 * DH] = kb_.astype(BF16)
        vb[s, j, p, 0:DH] = va.astype(BF16)
        vb[s, j, p, DH : 2 * DH] = vb_.astype(BF16)

    def dot(x, y):
        return jnp.dot(x, y, preferred_element_type=F32)

    middle = lax.broadcasted_iota(jnp.int32, (1, DH), 1) < HALF - DH

    def weigh(scores, top, values):
        weights = jnp.exp((scores - top) * SCALE)
        total = jnp.sum(weights, axis=0, keepdims=True)
        rounded = weights.astype(BF16)
        both = dot(values, rounded[:, : 2 * DH])
        last = dot(values[DH:], rounded[:, 2 * DH :])
        out = jnp.concatenate(
            [both[:DH, :DH], jnp.where(middle, both[:DH, DH:], both[DH:, DH:]), last], axis=1
        )
        return total, out

    def highest(scores):
        return jnp.max(scores, axis=0, keepdims=True)

    def loop(body, both):
        def step(p, carry):
            if both:
                done = [body(p), body(p + PAIRS // 2)]
            else:
                done = [body(p)]
            for store in done:
                if store is not None:
                    store()
            return carry

        lax.fori_loop(0, PAIRS // 2 if both else PAIRS, step, 0)

    def build_half(s, j):
        prep_b(s, j)
        loop(lambda p: build_kv(s, j, p), False)

    def put(which, p, state):
        m_acc[which, p], l_acc[which, p], o_acc[which, p] = state

    def get(which, p):
        return m_acc[which, p], l_acc[which, p], o_acc[which, p]

    def own_position(p):
        k_low, v_low = kb[0, jl0, p], vb[0, jl0, p]
        k_high, v_high = kb[0, 1 - jl0, p], vb[0, 1 - jl0, p]
        q_low, q_high = qbd[jl0, p], qbd[1 - jl0, p]
        shape = (HALF, 2 * HALF)
        row = lax.broadcasted_iota(jnp.int32, shape, 0)
        col = lax.broadcasted_iota(jnp.int32, shape, 1)
        seen = row <= jnp.where(col < HALF, col, col - HALF)
        low = jnp.where(seen, dot(k_low, q_low), MASKED)
        cross = dot(k_low, q_high)
        high = jnp.where(seen, dot(k_high, q_high), MASKED)
        m_low = highest(low)
        m_high = jnp.maximum(highest(cross), highest(high))
        l_low, o_low = weigh(low, m_low, v_low)
        l_cross, o_cross = weigh(cross, m_high, v_low)
        l_high, o_high = weigh(high, m_high, v_high)

        def store():
            put(0, p, (m_low, l_low, o_low))
            put(1, p, (m_high, l_cross + l_high, o_cross + o_high))

        return store

    def earlier_position(s, last=False):
        jls, lows = scalars(s)
        pick = (lows > low0).astype(jnp.int32)
        jq = jl0 + pick - 2 * jl0 * pick
        jk = jls + pick - 2 * jls * pick
        is_high = pick == 1

        def body(p):
            m_low, l_low, o_low = get(0, p)
            m_high, l_high, o_high = get(1, p)
            k1, v1, q1 = kb[s, jls, p], vb[s, jls, p], qbd[1 - jl0, p]
            k2, v2, q2 = kb[s, jk, p], vb[s, jk, p], qbd[jq, p]
            s1 = dot(k1, q1)
            s2 = dot(k2, q2)
            top1, top2 = highest(s1), highest(s2)
            high = jnp.maximum(jnp.maximum(m_high, top1), jnp.where(is_high, top2, MASKED))
            low = jnp.maximum(m_low, jnp.where(is_high, MASKED, top2))
            t1, o1 = weigh(s1, high, v1)
            t2, o2 = weigh(s2, jnp.where(is_high, high, low), v2)
            r_high = jnp.exp((m_high - high) * SCALE)
            r_low = jnp.exp((m_low - low) * SCALE)
            l_high = l_high * r_high + t1 + jnp.where(is_high, t2, 0.0)
            l_low = l_low * r_low + jnp.where(is_high, 0.0, t2)
            o_high = o_high * r_high + o1 + jnp.where(is_high, o2, 0.0)
            o_low = o_low * r_low + jnp.where(is_high, 0.0, o2)

            def store():
                if not last:
                    put(0, p, (low, l_low, o_low))
                    put(1, p, (high, l_high, o_high))
                    return
                rows_low = (o_low * (0.5 / l_low)).T.astype(BF16)
                rows_high = (o_high * (0.5 / l_high)).T.astype(BF16)
                log_low = low * SCALE + jnp.log(l_low)
                log_high = high * SCALE + jnp.log(l_high)
                for j in range(2):
                    is_low = jl0 == j
                    rows = jnp.where(is_low, rows_low, rows_high)
                    out_ref[p, j * HALF : (j + 1) * HALF, :] = rows[:HALF]
                    out_ref[p + PAIRS, j * HALF : (j + 1) * HALF, :] = rows[HALF:]
                    logs[j, pl.ds(p, 1), :] = jnp.where(is_low, log_low, log_high)
                for head in (p, p + PAIRS):
                    write_out(head).start()

            return store

        loop(body, True)

    def write_out(head):
        return pltpu.make_async_copy(out_ref.at[head], out_hbm.at[head], out_sem.at[head])

    jl0, low0 = scalars(0)
    prep_a(0)
    build_half(0, h)
    prep_aq()
    prep_q(h)
    ex_kv.wait_recv()
    first_sends(b_copies)
    loop(lambda p: build_q(h, p), False)
    wait_a(1)
    forward_one(a_copies)
    build_half(0, other)
    prep_a(1)
    build_half(1, h)
    wait_b(1)
    forward_one(b_copies)
    build_half(1, other)
    wait_a(2)
    forward_two(a_copies)
    prep_a(2)
    build_half(2, h)
    ex_q.wait_recv()
    prep_q(other)
    loop(lambda p: build_q(other, p), False)
    loop(own_position, True)
    wait_b(2)
    forward_two(b_copies)
    earlier_position(1)
    build_half(2, other)
    earlier_position(2)
    wait_a(3)
    prep_a(3)
    build_half(3, h)
    wait_b(3)
    build_half(3, other)
    earlier_position(3, last=True)
    log0, log1 = logs[0], logs[1]
    log_ref[0:PAIRS] = jnp.where(first, log0, pltpu.roll(log1, HALF, 1))
    log_ref[PAIRS:] = jnp.where(first, pltpu.roll(log0, HALF, 1), log1)

    write_log = pltpu.make_async_copy(log_ref, log_hbm, out_sem.at[2 * PAIRS])
    write_log.start()

    ex_kv.wait_send()
    ex_q.wait_send()
    for copies in (a_copies, b_copies):
        for copy in copies(0, 0, 1, near):
            copy.wait_send()

    @pl.when(core == 0)
    def _():
        for copies in (a_copies, b_copies):
            for slot in range(1, 5):
                for copy in copies(slot, 0, 1, near):
                    copy.wait_send()

    for head in range(2 * PAIRS):
        write_out(head).wait()
    write_log.wait()


def on_device(block_table, a_query, b_query, a_key, b_key, a_value, b_value):
    rows = 2 * HALF
    heads = 2 * PAIRS
    hbm = pl.BlockSpec(memory_space=pltpu.HBM)
    dma = pltpu.SemaphoreType.DMA
    return pl.pallas_call(
        kernel,
        out_shape=(
            jax.ShapeDtypeStruct((heads, rows, DH), BF16),
            jax.ShapeDtypeStruct((heads, rows), F32),
        ),
        in_specs=[pl.BlockSpec(memory_space=pltpu.SMEM)] + [hbm] * 6,
        out_specs=(hbm, hbm),
        scratch_shapes=[
            pltpu.VMEM((heads, rows, DH), BF16),
            pltpu.VMEM((heads, rows), F32),
            pltpu.VMEM((4, 8, 128), jnp.int32),
            pltpu.SMEM((4, 8, 128), jnp.int32),
            pltpu.VMEM((RQ, heads, rows), BF16),
            pltpu.VMEM((2, HALF, RQ * DH), BF16),
            pltpu.VMEM((4, 2, 2, HALF, 2 * DH), BF16),
            pltpu.VMEM((4, 4, heads, rows), BF16),
            pltpu.VMEM((2, RQ * DH, rows), BF16),
            pltpu.VMEM((2, RQ, PAIRS, rows), F32),
            pltpu.VMEM((2, PAIRS, 2 * DH, rows), BF16),
            pltpu.VMEM((4, 2, HALF, 2 * DH), F32),
            pltpu.VMEM((4, 2, 2 * DH, HALF), F32),
            pltpu.VMEM((4, 2, HALF, 128), F32),
            pltpu.VMEM((4, 2, 2, heads, HALF), F32),
            pltpu.VMEM((4, 2, PAIRS, HALF, 2 * DH), BF16),
            pltpu.VMEM((4, 2, PAIRS, 2 * DH, HALF), BF16),
            pltpu.VMEM((2, PAIRS, DH, rows), F32),
            pltpu.VMEM((2, PAIRS, 1, rows), F32),
            pltpu.VMEM((2, PAIRS, 1, rows), F32),
            pltpu.VMEM((2, PAIRS, rows), F32),
            dma((heads + 1,)),
            dma((6,)),
            dma((4,)),
            dma((2,)),
            dma((2,)),
            dma((5,)),
            dma((3,)),
            dma((5,)),
            dma((3,)),
            dma((5,)),
            dma((3,)),
            dma((5,)),
            dma((3,)),
        ],
        compiler_params=pltpu.CompilerParams(
            collective_id=0, has_side_effects=True, vmem_limit_bytes=60 * 1024 * 1024
        ),
    )(block_table, a_query, b_query, a_key, b_key, a_value, b_value)


def solution(mesh):
    in_specs = (
        P("blk", None),
        P(None, "head", "blk"),
        P(("blk", "head"), None),
        P(None, "head", "blk"),
        P(("blk", "head"), None),
        P(None, "head", "blk"),
        P(("blk", "head"), None),
    )
    out_specs = (P("head", "blk", None), P("head", "blk"))
    return jax.shard_map(
        on_device, mesh=mesh, in_specs=in_specs, out_specs=out_specs, check_vma=False
    )
```

```python
import math

import jax
import jax.numpy as jnp
from jax import lax
from jax.experimental import pallas as pl
from jax.experimental.pallas import tpu as pltpu
from jax.sharding import PartitionSpec as P

HALF = 192
DH = 128
PAIRS = 8
RQ = 6
MESH = pl.DeviceIdType.MESH
F32 = jnp.float32
BF16 = jnp.bfloat16
SCALE = 0.5 / math.sqrt(DH)
MASKED = -1e30


def kernel(
    bt_in, aq_in, bq_in, ak_in, bk_in, av_in, bv_in,
    out_hbm, log_hbm,
    relay_kv, relay_q, out_ref, log_ref, bt, bts, aq, bq, bkv, akv,
    bqt, a2q, qbd, bkf, bvt, akt, avj, kb, vb,
    o_acc, m_acc, l_acc, logs,
    out_sem, local_sem, bts_sem, ex_send, ex_recv, a_send, a_recv, f_send, f_recv, t_send, t_recv, b_send, b_recv,
):
    e = lax.axis_index("blk")
    h = lax.axis_index("head")
    places = lax.axis_size("blk")
    other = 1 - h
    core = lax.rem(e, 2)
    lane = lax.broadcasted_iota(jnp.int32, (1, 2 * HALF), 1)
    first = lane < HALF

    def at(blk, head):
        return {"blk": lax.rem(blk + places, places), "head": head}

    across = e + places // 2
    chip = lax.rem(e // 2, places // 4)
    leaves = chip == places // 4 - 1
    enters = jnp.logical_and(chip == 0, core == 0)

    barrier = pltpu.get_barrier_semaphore()

    def greet(target):
        pl.semaphore_signal(barrier, inc=1, device_id=target, device_id_type=MESH)

    greet(at(across, h))
    greet(at(across, other))
    greet(at(e - 1, h))

    @pl.when(core == 0)
    def _():
        greet(at(e - 2, h))

    @pl.when(enters)
    def _():
        greet(at(e - 1, other))
        greet(at(e - 2, other))

    locals_ = [
        pltpu.make_async_copy(src, dst, local_sem.at[i])
        for i, (src, dst) in enumerate(
            [
                (bk_in, bkv.at[0, h, 0]),
                (bv_in, bkv.at[0, h, 1]),
                (ak_in, akv.at[0, pl.ds(0, 2)]),
                (av_in, akv.at[0, pl.ds(2, 2)]),
                (bq_in, bq.at[h]),
                (aq_in, aq),
            ]
        )
    ]
    for copy in locals_:
        copy.start()
    own0, own1 = bt_in[0, 0], bt_in[0, 1]
    tlane = lax.broadcasted_iota(jnp.int32, (8, 128), 1)
    bt[0] = jnp.where(tlane == 0, own0, own1)

    pl.semaphore_wait(barrier, 4 - core + leaves.astype(jnp.int32))

    def remote(src, dst, send, recv, target):
        return pltpu.make_async_remote_copy(
            src_ref=src, dst_ref=dst, send_sem=send, recv_sem=recv, device_id=target, device_id_type=MESH
        )

    def a_copies(slot, s_from, s_to, target):
        to = target[0]
        return [
            remote(bkv.at[s_from, h], bkv.at[s_to, h], a_send.at[slot], a_recv.at[s_to - 1], to),
            remote(akv.at[s_from], akv.at[s_to], f_send.at[slot], f_recv.at[s_to - 1], to),
            remote(bt.at[s_from], bt.at[s_to], t_send.at[slot], t_recv.at[s_to - 1], to),
        ]

    def b_copies(slot, s_from, s_to, target):
        _, half, to = target
        return [remote(bkv.at[s_from, half], bkv.at[s_to, half], b_send.at[slot], b_recv.at[s_to - 1], to)]

    def ahead(by, turns):
        half = jnp.where(turns, h, other)
        return at(e + by, h), half, at(e + by, 1 - half)

    near = ahead(1, jnp.logical_and(leaves, core == 1))
    far = ahead(2, leaves)
    def start(copies):
        for copy in copies:
            copy.start()

    def first_sends(copies):
        start(copies(0, 0, 1, near))

    def forward_one(copies):
        @pl.when(core == 0)
        def _():
            start(copies(1, 1, 2, near))
            start(copies(2, 0, 2, far))
            start(copies(3, 1, 3, far))

    def forward_two(copies):
        @pl.when(core == 0)
        def _():
            start(copies(4, 2, 3, near))

    def wait_a(s):
        for copy in a_copies(0, s - 1, s, near):
            copy.wait_recv()

    def wait_b(s):
        for copy in b_copies(0, s - 1, s, (near[0], other, near[0])):
            copy.wait_recv()

    same, cross = at(across, h), at(across, other)
    half_rows = HALF // 2

    def q_part(half, i):
        return bq.at[half, pl.ds(i * half_rows, half_rows)]

    def out_copy(i, src, dst, target):
        return remote(src, dst, ex_send.at[i], ex_recv.at[i], target)

    kv_out = [
        out_copy(0, bkv.at[0, h, 0], relay_kv.at[0], same),
        out_copy(1, bkv.at[0, h, 1], relay_kv.at[1], cross),
    ]
    q_out = [
        out_copy(2, q_part(h, 0), relay_q.at[0], same),
        out_copy(3, q_part(h, 1), relay_q.at[1], cross),
    ]
    kv_on = [
        out_copy(4, relay_kv.at[0], bkv.at[0, h, 0], cross),
        out_copy(5, relay_kv.at[1], bkv.at[0, other, 1], same),
    ]
    q_on = [
        out_copy(6, relay_q.at[0], q_part(h, 0), cross),
        out_copy(7, relay_q.at[1], q_part(other, 1), same),
    ]

    def pass_on(arrived, onward):
        for before, after in zip(arrived, onward):
            before.wait_recv()
            after.start()

    def wait_all(copies):
        for copy in copies:
            copy.wait_recv()

    for copy in locals_[:4]:
        copy.wait()
    start(kv_out)
    first_sends(a_copies)
    locals_[4].wait()
    start(q_out)
    locals_[5].wait()

    def scalars(s):
        copy = pltpu.make_async_copy(bt.at[s], bts.at[s], bts_sem.at[s])
        copy.start()
        copy.wait()
        b0, b1 = bts[s, 0, 0], bts[s, 0, 1]
        return (b0 > b1).astype(jnp.int32), jnp.minimum(b0, b1)

    def prep_a(s):
        x = akv[s].astype(F32)
        keys = x[0:2].reshape(32, 2 * HALF)
        keys_t = jnp.concatenate([keys, jnp.zeros((96, 2 * HALF), F32)], axis=0).T
        akt[s, 0] = keys_t[:HALF]
        akt[s, 1] = keys_t[HALF:]
        avj[s, 0] = x[2:4, :, :HALF]
        avj[s, 1] = x[2:4, :, HALF:]

    def prep_b(s, j):
        bkf[s, j] = bkv[s, j, 0].astype(F32)
        v = bkv[s, j, 1].astype(F32)
        v = jnp.concatenate([v, jnp.zeros((64, 2 * DH), F32)], axis=0).T
        bvt[s, j] = v[:, :HALF]

    def prep_q(j):
        b = bq[j].astype(F32)
        bqt[j] = jnp.concatenate([b, b], axis=0).T.astype(BF16)

    def prep_aq():
        x = aq[...].astype(F32)
        low, high = x[:, :PAIRS], x[:, PAIRS:]
        wide = first[None]

        def turned(y):
            return pltpu.roll(y.reshape(RQ * PAIRS, 2 * HALF), HALF, 1).reshape(y.shape)

        a2q[0] = jnp.where(wide, low, turned(high))
        a2q[1] = jnp.where(wide, turned(low), high)

    def build_q(j, p):
        total = a2q[j, 0, pl.ds(p, 1), :] * bqt[j, 0:DH, :].astype(F32)
        for r in range(1, RQ):
            total += a2q[j, r, pl.ds(p, 1), :] * bqt[j, r * DH : (r + 1) * DH, :].astype(F32)
        total = total * (1.0 / RQ)
        qbd[j, p, 0:DH] = jnp.where(first, total, 0.0).astype(BF16)
        qbd[j, p, DH : 2 * DH] = jnp.where(first, 0.0, total).astype(BF16)

    def build_kv(s, j, p):
        a = pltpu.roll(akt[s, j], lax.rem(128 - p, 128), 1)
        b0, b1 = bkf[s, j, :, 0:DH], bkf[s, j, :, DH : 2 * DH]
        ka = a[:, 0:1] * b0 + a[:, 16:17] * b1
        kb_ = a[:, 8:9] * b0 + a[:, 24:25] * b1
        c0, c1 = bvt[s, j, 0:DH], bvt[s, j, DH : 2 * DH]
        va = avj[s, j, 0, pl.ds(p, 1), :] * c0 + avj[s, j, 1, pl.ds(p, 1), :] * c1
        vb_ = avj[s, j, 0, pl.ds(p + PAIRS, 1), :] * c0 + avj[s, j, 1, pl.ds(p + PAIRS, 1), :] * c1
        kb[s, j, p, :, 0:DH] = ka.astype(BF16)
        kb[s, j, p, :, DH : 2 * DH] = kb_.astype(BF16)
        vb[s, j, p, 0:DH] = va.astype(BF16)
        vb[s, j, p, DH : 2 * DH] = vb_.astype(BF16)

    def dot(x, y):
        return jnp.dot(x, y, preferred_element_type=F32)

    middle = lax.broadcasted_iota(jnp.int32, (1, DH), 1) < HALF - DH

    def weigh(scores, top, values):
        weights = jnp.exp((scores - top) * SCALE)
        total = jnp.sum(weights, axis=0, keepdims=True)
        rounded = weights.astype(BF16)
        both = dot(values, rounded[:, : 2 * DH])
        last = dot(values[DH:], rounded[:, 2 * DH :])
        out = jnp.concatenate(
            [both[:DH, :DH], jnp.where(middle, both[:DH, DH:], both[DH:, DH:]), last], axis=1
        )
        return total, out

    def highest(scores):
        return jnp.max(scores, axis=0, keepdims=True)

    def loop(body, both):
        def step(p, carry):
            if both:
                done = [body(p), body(p + PAIRS // 2)]
            else:
                done = [body(p)]
            for store in done:
                if store is not None:
                    store()
            return carry

        lax.fori_loop(0, PAIRS // 2 if both else PAIRS, step, 0)

    def build_half(s, j):
        prep_b(s, j)
        loop(lambda p: build_kv(s, j, p), False)

    def put(which, p, state):
        m_acc[which, p], l_acc[which, p], o_acc[which, p] = state

    def get(which, p):
        return m_acc[which, p], l_acc[which, p], o_acc[which, p]

    def own_position(p):
        k_low, v_low = kb[0, jl0, p], vb[0, jl0, p]
        k_high, v_high = kb[0, 1 - jl0, p], vb[0, 1 - jl0, p]
        q_low, q_high = qbd[jl0, p], qbd[1 - jl0, p]
        shape = (HALF, 2 * HALF)
        row = lax.broadcasted_iota(jnp.int32, shape, 0)
        col = lax.broadcasted_iota(jnp.int32, shape, 1)
        seen = row <= jnp.where(col < HALF, col, col - HALF)
        low = jnp.where(seen, dot(k_low, q_low), MASKED)
        cross = dot(k_low, q_high)
        high = jnp.where(seen, dot(k_high, q_high), MASKED)
        m_low = highest(low)
        m_high = jnp.maximum(highest(cross), highest(high))
        l_low, o_low = weigh(low, m_low, v_low)
        l_cross, o_cross = weigh(cross, m_high, v_low)
        l_high, o_high = weigh(high, m_high, v_high)

        def store():
            put(0, p, (m_low, l_low, o_low))
            put(1, p, (m_high, l_cross + l_high, o_cross + o_high))

        return store

    def earlier_position(s, last=False):
        jls, lows = scalars(s)
        pick = (lows > low0).astype(jnp.int32)
        jq = jl0 + pick - 2 * jl0 * pick
        jk = jls + pick - 2 * jls * pick
        is_high = pick == 1

        def body(p):
            m_low, l_low, o_low = get(0, p)
            m_high, l_high, o_high = get(1, p)
            k1, v1, q1 = kb[s, jls, p], vb[s, jls, p], qbd[1 - jl0, p]
            k2, v2, q2 = kb[s, jk, p], vb[s, jk, p], qbd[jq, p]
            s1 = dot(k1, q1)
            s2 = dot(k2, q2)
            top1, top2 = highest(s1), highest(s2)
            high = jnp.maximum(jnp.maximum(m_high, top1), jnp.where(is_high, top2, MASKED))
            low = jnp.maximum(m_low, jnp.where(is_high, MASKED, top2))
            t1, o1 = weigh(s1, high, v1)
            t2, o2 = weigh(s2, jnp.where(is_high, high, low), v2)
            r_high = jnp.exp((m_high - high) * SCALE)
            r_low = jnp.exp((m_low - low) * SCALE)
            l_high = l_high * r_high + t1 + jnp.where(is_high, t2, 0.0)
            l_low = l_low * r_low + jnp.where(is_high, 0.0, t2)
            o_high = o_high * r_high + o1 + jnp.where(is_high, o2, 0.0)
            o_low = o_low * r_low + jnp.where(is_high, 0.0, o2)

            def store():
                if not last:
                    put(0, p, (low, l_low, o_low))
                    put(1, p, (high, l_high, o_high))
                    return
                rows_low = (o_low * (0.5 / l_low)).T.astype(BF16)
                rows_high = (o_high * (0.5 / l_high)).T.astype(BF16)
                log_low = low * SCALE + jnp.log(l_low)
                log_high = high * SCALE + jnp.log(l_high)
                for j in range(2):
                    is_low = jl0 == j
                    rows = jnp.where(is_low, rows_low, rows_high)
                    out_ref[p, j * HALF : (j + 1) * HALF, :] = rows[:HALF]
                    out_ref[p + PAIRS, j * HALF : (j + 1) * HALF, :] = rows[HALF:]
                    logs[j, pl.ds(p, 1), :] = jnp.where(is_low, log_low, log_high)
                for head in (p, p + PAIRS):
                    write_out(head).start()

            return store

        loop(body, True)

    def write_out(head):
        return pltpu.make_async_copy(out_ref.at[head], out_hbm.at[head], out_sem.at[head])

    jl0, low0 = scalars(0)
    prep_a(0)
    build_half(0, h)
    prep_aq()
    pass_on(kv_out, kv_on)
    prep_q(h)
    wait_a(1)
    forward_one(a_copies)
    loop(lambda p: build_q(h, p), False)
    wait_all(kv_on)
    first_sends(b_copies)
    build_half(0, other)
    pass_on(q_out, q_on)
    prep_a(1)
    build_half(1, h)
    wait_b(1)
    forward_one(b_copies)
    build_half(1, other)
    wait_a(2)
    forward_two(a_copies)
    prep_a(2)
    build_half(2, h)
    wait_all(q_on)
    prep_q(other)
    loop(lambda p: build_q(other, p), False)
    loop(own_position, True)
    wait_b(2)
    forward_two(b_copies)
    earlier_position(1)
    build_half(2, other)
    earlier_position(2)
    wait_a(3)
    prep_a(3)
    build_half(3, h)
    wait_b(3)
    build_half(3, other)
    earlier_position(3, last=True)
    log0, log1 = logs[0], logs[1]
    log_ref[0:PAIRS] = jnp.where(first, log0, pltpu.roll(log1, HALF, 1))
    log_ref[PAIRS:] = jnp.where(first, pltpu.roll(log0, HALF, 1), log1)

    write_log = pltpu.make_async_copy(log_ref, log_hbm, out_sem.at[2 * PAIRS])
    write_log.start()

    for copy in kv_out + q_out + kv_on + q_on:
        copy.wait_send()
    for copies in (a_copies, b_copies):
        for copy in copies(0, 0, 1, near):
            copy.wait_send()

    @pl.when(core == 0)
    def _():
        for copies in (a_copies, b_copies):
            for slot in range(1, 5):
                for copy in copies(slot, 0, 1, near):
                    copy.wait_send()

    for head in range(2 * PAIRS):
        write_out(head).wait()
    write_log.wait()


def on_device(block_table, a_query, b_query, a_key, b_key, a_value, b_value):
    rows = 2 * HALF
    heads = 2 * PAIRS
    hbm = pl.BlockSpec(memory_space=pltpu.HBM)
    dma = pltpu.SemaphoreType.DMA
    return pl.pallas_call(
        kernel,
        out_shape=(
            jax.ShapeDtypeStruct((heads, rows, DH), BF16),
            jax.ShapeDtypeStruct((heads, rows), F32),
        ),
        in_specs=[pl.BlockSpec(memory_space=pltpu.SMEM)] + [hbm] * 6,
        out_specs=(hbm, hbm),
        scratch_shapes=[
            pltpu.VMEM((2, HALF, 2 * DH), BF16),
            pltpu.VMEM((2, HALF // 2, RQ * DH), BF16),
            pltpu.VMEM((heads, rows, DH), BF16),
            pltpu.VMEM((heads, rows), F32),
            pltpu.VMEM((4, 8, 128), jnp.int32),
            pltpu.SMEM((4, 8, 128), jnp.int32),
            pltpu.VMEM((RQ, heads, rows), BF16),
            pltpu.VMEM((2, HALF, RQ * DH), BF16),
            pltpu.VMEM((4, 2, 2, HALF, 2 * DH), BF16),
            pltpu.VMEM((4, 4, heads, rows), BF16),
            pltpu.VMEM((2, RQ * DH, rows), BF16),
            pltpu.VMEM((2, RQ, PAIRS, rows), F32),
            pltpu.VMEM((2, PAIRS, 2 * DH, rows), BF16),
            pltpu.VMEM((4, 2, HALF, 2 * DH), F32),
            pltpu.VMEM((4, 2, 2 * DH, HALF), F32),
            pltpu.VMEM((4, 2, HALF, 128), F32),
            pltpu.VMEM((4, 2, 2, heads, HALF), F32),
            pltpu.VMEM((4, 2, PAIRS, HALF, 2 * DH), BF16),
            pltpu.VMEM((4, 2, PAIRS, 2 * DH, HALF), BF16),
            pltpu.VMEM((2, PAIRS, DH, rows), F32),
            pltpu.VMEM((2, PAIRS, 1, rows), F32),
            pltpu.VMEM((2, PAIRS, 1, rows), F32),
            pltpu.VMEM((2, PAIRS, rows), F32),
            dma((heads + 1,)),
            dma((6,)),
            dma((4,)),
            dma((8,)),
            dma((8,)),
            dma((5,)),
            dma((3,)),
            dma((5,)),
            dma((3,)),
            dma((5,)),
            dma((3,)),
            dma((5,)),
            dma((3,)),
        ],
        compiler_params=pltpu.CompilerParams(
            collective_id=0, has_side_effects=True, vmem_limit_bytes=60 * 1024 * 1024
        ),
    )(block_table, a_query, b_query, a_key, b_key, a_value, b_value)


def solution(mesh):
    in_specs = (
        P("blk", None),
        P(None, "head", "blk"),
        P(("blk", "head"), None),
        P(None, "head", "blk"),
        P(("blk", "head"), None),
        P(None, "head", "blk"),
        P(("blk", "head"), None),
    )
    out_specs = (P("head", "blk", None), P("head", "blk"))
    return jax.shard_map(
        on_device, mesh=mesh, in_specs=in_specs, out_specs=out_specs, check_vma=False
    )
```

```python
import math

import jax
import jax.numpy as jnp
from jax import lax
from jax.experimental import pallas as pl
from jax.experimental.pallas import tpu as pltpu
from jax.sharding import PartitionSpec as P

HALF = 192
DH = 128
PAIRS = 8
RQ = 6
MESH = pl.DeviceIdType.MESH
F32 = jnp.float32
BF16 = jnp.bfloat16
SCALE = 0.5 / math.sqrt(DH)
MASKED = -1e30


def kernel(
    bt_in, aq_in, bq_in, ak_in, bk_in, av_in, bv_in,
    out_hbm, log_hbm,
    relay_kv, relay_q, out_ref, log_ref, bt, bts, aq, bq, bkv, akv,
    bqt, a2q, qbd, bkf, bvt, akt, avj, kb, vb,
    o_acc, m_acc, l_acc, logs, ident, spread,
    out_sem, local_sem, bts_sem, ex_send, ex_recv, a_send, a_recv, f_send, f_recv, t_send, t_recv, b_send, b_recv,
):
    e = lax.axis_index("blk")
    h = lax.axis_index("head")
    places = lax.axis_size("blk")
    other = 1 - h
    core = lax.rem(e, 2)
    lane = lax.broadcasted_iota(jnp.int32, (1, 2 * HALF), 1)
    first = lane < HALF

    def at(blk, head):
        return {"blk": lax.rem(blk + places, places), "head": head}

    across = e + places // 2
    chip = lax.rem(e // 2, places // 4)
    leaves = chip == places // 4 - 1
    enters = jnp.logical_and(chip == 0, core == 0)

    barrier = pltpu.get_barrier_semaphore()

    def greet(target):
        pl.semaphore_signal(barrier, inc=1, device_id=target, device_id_type=MESH)

    greet(at(across, h))
    greet(at(across, other))
    greet(at(e - 1, h))

    @pl.when(core == 0)
    def _():
        greet(at(e - 2, h))

    @pl.when(enters)
    def _():
        greet(at(e - 1, other))
        greet(at(e - 2, other))

    locals_ = [
        pltpu.make_async_copy(src, dst, local_sem.at[i])
        for i, (src, dst) in enumerate(
            [
                (bk_in, bkv.at[0, h, 0]),
                (bv_in, bkv.at[0, h, 1]),
                (ak_in, akv.at[0, pl.ds(0, 2)]),
                (av_in, akv.at[0, pl.ds(2, 2)]),
                (bq_in, bq.at[h]),
                (aq_in, aq),
            ]
        )
    ]
    for copy in locals_:
        copy.start()
    side = (2 * DH, 2 * DH)
    ident[...] = (
        lax.broadcasted_iota(jnp.int32, side, 0) == lax.broadcasted_iota(jnp.int32, side, 1)
    ).astype(F32).astype(BF16)
    side = (4 * PAIRS, 4 * DH)
    source = lax.broadcasted_iota(jnp.int32, side, 0)
    wanted = lax.broadcasted_iota(jnp.int32, side, 1) // DH * PAIRS
    for p in range(PAIRS):
        spread[p] = (source == wanted + p).astype(F32).astype(BF16)
    own0, own1 = bt_in[0, 0], bt_in[0, 1]
    tlane = lax.broadcasted_iota(jnp.int32, (8, 128), 1)
    bt[0] = jnp.where(tlane == 0, own0, own1)

    pl.semaphore_wait(barrier, 4 - core + leaves.astype(jnp.int32))

    def remote(src, dst, send, recv, target):
        return pltpu.make_async_remote_copy(
            src_ref=src, dst_ref=dst, send_sem=send, recv_sem=recv, device_id=target, device_id_type=MESH
        )

    def a_copies(slot, s_from, s_to, target):
        to = target[0]
        return [
            remote(bkv.at[s_from, h], bkv.at[s_to, h], a_send.at[slot], a_recv.at[s_to - 1], to),
            remote(akv.at[s_from], akv.at[s_to], f_send.at[slot], f_recv.at[s_to - 1], to),
            remote(bt.at[s_from], bt.at[s_to], t_send.at[slot], t_recv.at[s_to - 1], to),
        ]

    def b_copies(slot, s_from, s_to, target):
        _, half, to = target
        return [remote(bkv.at[s_from, half], bkv.at[s_to, half], b_send.at[slot], b_recv.at[s_to - 1], to)]

    def ahead(by, turns):
        half = jnp.where(turns, h, other)
        return at(e + by, h), half, at(e + by, 1 - half)

    near = ahead(1, jnp.logical_and(leaves, core == 1))
    far = ahead(2, leaves)
    def start(copies):
        for copy in copies:
            copy.start()

    last_core = jnp.logical_and(leaves, core == 1)
    last_first = jnp.logical_and(leaves, core == 0)

    def first_a():
        start(a_copies(0, 0, 1, near))

        @pl.when(last_core)
        def _():
            start(b_copies(0, 0, 1, near))

    def first_b():
        @pl.when(jnp.logical_not(last_core))
        def _():
            start(b_copies(0, 0, 1, near))

    def forward_a():
        @pl.when(core == 0)
        def _():
            start(a_copies(1, 1, 2, near))
            start(a_copies(2, 0, 2, far))
            start(a_copies(3, 1, 3, far))

        @pl.when(last_first)
        def _():
            start(b_copies(2, 0, 2, far))
            start(b_copies(3, 1, 3, far))

    def forward_b():
        @pl.when(core == 0)
        def _():
            start(b_copies(1, 1, 2, near))

        @pl.when(jnp.logical_and(core == 0, jnp.logical_not(leaves)))
        def _():
            start(b_copies(2, 0, 2, far))
            start(b_copies(3, 1, 3, far))

    def forward_two(copies):
        @pl.when(core == 0)
        def _():
            start(copies(4, 2, 3, near))

    def wait_a(s):
        for copy in a_copies(0, s - 1, s, near):
            copy.wait_recv()

    def wait_b(s):
        for copy in b_copies(0, s - 1, s, (near[0], other, near[0])):
            copy.wait_recv()

    same, cross = at(across, h), at(across, other)
    half_rows = HALF // 2

    def q_part(half, i):
        return bq.at[half, pl.ds(i * half_rows, half_rows)]

    def out_copy(i, src, dst, target):
        return remote(src, dst, ex_send.at[i], ex_recv.at[i], target)

    kv_out = [
        out_copy(0, bkv.at[0, h, 0], relay_kv.at[0], same),
        out_copy(1, bkv.at[0, h, 1], relay_kv.at[1], cross),
    ]
    q_out = [
        out_copy(2, q_part(h, 0), relay_q.at[0], same),
        out_copy(3, q_part(h, 1), relay_q.at[1], cross),
    ]
    kv_on = [
        out_copy(4, relay_kv.at[0], bkv.at[0, h, 0], cross),
        out_copy(5, relay_kv.at[1], bkv.at[0, other, 1], same),
    ]
    q_on = [
        out_copy(6, relay_q.at[0], q_part(h, 0), cross),
        out_copy(7, relay_q.at[1], q_part(other, 1), same),
    ]

    def pass_on(arrived, onward):
        for before, after in zip(arrived, onward):
            before.wait_recv()
            after.start()

    def wait_all(copies):
        for copy in copies:
            copy.wait_recv()

    for copy in locals_[:4]:
        copy.wait()
    start(kv_out)
    first_a()
    locals_[4].wait()
    start(q_out)
    locals_[5].wait()

    def scalars(s):
        copy = pltpu.make_async_copy(bt.at[s], bts.at[s], bts_sem.at[s])
        copy.start()
        copy.wait()
        b0, b1 = bts[s, 0, 0], bts[s, 0, 1]
        return (b0 > b1).astype(jnp.int32), jnp.minimum(b0, b1)

    def dot(x, y):
        return jnp.dot(x, y, preferred_element_type=F32)

    def turn(y):
        n = y.shape[1]
        return lax.dot_general(ident[:n, :n], y, (((1,), (1,)), ((), ())), preferred_element_type=F32)

    def prep_a(s):
        keys = akv[s, 0:2].reshape(4 * PAIRS, 2 * HALF)
        keys_t = jnp.concatenate([turn(keys[:, i * DH : (i + 1) * DH]) for i in range(3)], axis=0)
        akt[s, 0] = keys_t[:HALF].astype(BF16)
        akt[s, 1] = keys_t[HALF:].astype(BF16)
        values = akv[s, 2:4].astype(F32)
        avj[s, 0] = values[:, :, :HALF]
        avj[s, 1] = values[:, :, HALF:]

    def prep_b(s, j):
        bkf[s, j] = bkv[s, j, 0].astype(F32)
        bvt[s, j] = turn(bkv[s, j, 1])

    def prep_q(j):
        for i in range(RQ // 2):
            b = bq[j, :, i * 2 * DH : (i + 1) * 2 * DH]
            bqt[j, i * 2 * DH : (i + 1) * 2 * DH] = turn(jnp.concatenate([b, b], axis=0))

    def prep_aq():
        x = aq[...].astype(F32)
        low, high = x[:, :PAIRS], x[:, PAIRS:]
        wide = first[None]

        def turned(y):
            return pltpu.roll(y.reshape(RQ * PAIRS, 2 * HALF), HALF, 1).reshape(y.shape)

        a2q[0] = jnp.where(wide, low, turned(high))
        a2q[1] = jnp.where(wide, turned(low), high)

    def build_q(j, p):
        total = a2q[j, 0, pl.ds(p, 1), :] * bqt[j, 0:DH, :]
        for r in range(1, RQ):
            total += a2q[j, r, pl.ds(p, 1), :] * bqt[j, r * DH : (r + 1) * DH, :]
        total = total * (1.0 / RQ)
        qbd[j, p, 0:DH] = jnp.where(first, total, 0.0).astype(BF16)
        qbd[j, p, DH : 2 * DH] = jnp.where(first, 0.0, total).astype(BF16)

    def build_kv(s, j, p):
        wide = dot(akt[s, j], spread[p])
        b0, b1 = bkf[s, j, :, 0:DH], bkf[s, j, :, DH : 2 * DH]
        ka = wide[:, 0:DH] * b0 + wide[:, 2 * DH : 3 * DH] * b1
        kb_ = wide[:, DH : 2 * DH] * b0 + wide[:, 3 * DH :] * b1
        c0, c1 = bvt[s, j, 0:DH], bvt[s, j, DH : 2 * DH]
        va = avj[s, j, 0, pl.ds(p, 1), :] * c0 + avj[s, j, 1, pl.ds(p, 1), :] * c1
        vb_ = avj[s, j, 0, pl.ds(p + PAIRS, 1), :] * c0 + avj[s, j, 1, pl.ds(p + PAIRS, 1), :] * c1
        kb[s, j, p, :, 0:DH] = ka.astype(BF16)
        kb[s, j, p, :, DH : 2 * DH] = kb_.astype(BF16)
        vb[s, j, p, 0:DH] = va.astype(BF16)
        vb[s, j, p, DH : 2 * DH] = vb_.astype(BF16)

    middle = lax.broadcasted_iota(jnp.int32, (1, DH), 1) < HALF - DH

    def weigh(scores, top, values):
        weights = jnp.exp((scores - top) * SCALE)
        total = jnp.sum(weights, axis=0, keepdims=True)
        rounded = weights.astype(BF16)
        both = dot(values, rounded[:, : 2 * DH])
        last = dot(values[DH:], rounded[:, 2 * DH :])
        out = jnp.concatenate(
            [both[:DH, :DH], jnp.where(middle, both[:DH, DH:], both[DH:, DH:]), last], axis=1
        )
        return total, out

    def highest(scores):
        return jnp.max(scores, axis=0, keepdims=True)

    def loop(body, width):
        each = PAIRS // width

        def step(p, carry):
            done = [body(p + i * each) for i in range(width)]
            for store in done:
                if store is not None:
                    store()
            return carry

        lax.fori_loop(0, each, step, 0)

    def build_half(s, j):
        prep_b(s, j)
        loop(lambda p: build_kv(s, j, p), 4)

    def put(which, p, state):
        m_acc[which, p], l_acc[which, p], o_acc[which, p] = state

    def get(which, p):
        return m_acc[which, p], l_acc[which, p], o_acc[which, p]

    def own_position(p):
        k_low, v_low = kb[0, jl0, p], vb[0, jl0, p]
        k_high, v_high = kb[0, 1 - jl0, p], vb[0, 1 - jl0, p]
        q_low, q_high = qbd[jl0, p], qbd[1 - jl0, p]
        shape = (HALF, 2 * HALF)
        row = lax.broadcasted_iota(jnp.int32, shape, 0)
        col = lax.broadcasted_iota(jnp.int32, shape, 1)
        seen = row <= jnp.where(col < HALF, col, col - HALF)
        low = jnp.where(seen, dot(k_low, q_low), MASKED)
        cross = dot(k_low, q_high)
        high = jnp.where(seen, dot(k_high, q_high), MASKED)
        m_low = highest(low)
        m_high = jnp.maximum(highest(cross), highest(high))
        l_low, o_low = weigh(low, m_low, v_low)
        l_cross, o_cross = weigh(cross, m_high, v_low)
        l_high, o_high = weigh(high, m_high, v_high)

        def store():
            put(0, p, (m_low, l_low, o_low))
            put(1, p, (m_high, l_cross + l_high, o_cross + o_high))

        return store

    def earlier_position(s, last=False):
        jls, lows = scalars(s)
        pick = (lows > low0).astype(jnp.int32)
        jq = jl0 + pick - 2 * jl0 * pick
        jk = jls + pick - 2 * jls * pick
        is_high = pick == 1

        def body(p):
            m_low, l_low, o_low = get(0, p)
            m_high, l_high, o_high = get(1, p)
            k1, v1, q1 = kb[s, jls, p], vb[s, jls, p], qbd[1 - jl0, p]
            k2, v2, q2 = kb[s, jk, p], vb[s, jk, p], qbd[jq, p]
            s1 = dot(k1, q1)
            s2 = dot(k2, q2)
            top1, top2 = highest(s1), highest(s2)
            high = jnp.maximum(jnp.maximum(m_high, top1), jnp.where(is_high, top2, MASKED))
            low = jnp.maximum(m_low, jnp.where(is_high, MASKED, top2))
            t1, o1 = weigh(s1, high, v1)
            t2, o2 = weigh(s2, jnp.where(is_high, high, low), v2)
            r_high = jnp.exp((m_high - high) * SCALE)
            r_low = jnp.exp((m_low - low) * SCALE)
            l_high = l_high * r_high + t1 + jnp.where(is_high, t2, 0.0)
            l_low = l_low * r_low + jnp.where(is_high, 0.0, t2)
            o_high = o_high * r_high + o1 + jnp.where(is_high, o2, 0.0)
            o_low = o_low * r_low + jnp.where(is_high, 0.0, o2)

            def store():
                if not last:
                    put(0, p, (low, l_low, o_low))
                    put(1, p, (high, l_high, o_high))
                    return
                rows_low = turned_rows((o_low * (0.5 / l_low)).astype(BF16))
                rows_high = turned_rows((o_high * (0.5 / l_high)).astype(BF16))
                log_low = low * SCALE + jnp.log(l_low)
                log_high = high * SCALE + jnp.log(l_high)
                for j in range(2):
                    is_low = jl0 == j
                    rows = jnp.where(is_low, rows_low, rows_high)
                    out_ref[p, j * HALF : (j + 1) * HALF, :] = rows[:HALF]
                    out_ref[p + PAIRS, j * HALF : (j + 1) * HALF, :] = rows[HALF:]
                    logs[j, pl.ds(p, 1), :] = jnp.where(is_low, log_low, log_high)
                for head in (p, p + PAIRS):
                    write_out(head).start()

            return store

        loop(body, 2)

    def turned_rows(x):
        parts = [turn(x[:, i * DH : (i + 1) * DH]) for i in range(3)]
        return jnp.concatenate(parts, axis=0).astype(BF16)

    def write_out(head):
        return pltpu.make_async_copy(out_ref.at[head], out_hbm.at[head], out_sem.at[head])

    jl0, low0 = scalars(0)
    prep_a(0)
    prep_aq()
    build_half(0, h)
    pass_on(kv_out, kv_on)
    prep_q(h)
    loop(lambda p: build_q(h, p), 1)
    wait_a(1)
    forward_a()
    pass_on(q_out, q_on)
    wait_all(kv_on)
    first_b()
    build_half(0, other)
    prep_a(1)
    build_half(1, h)
    wait_b(1)
    forward_b()
    build_half(1, other)
    wait_a(2)
    forward_two(a_copies)
    prep_a(2)
    build_half(2, h)
    wait_all(q_on)
    prep_q(other)
    loop(lambda p: build_q(other, p), 1)
    loop(own_position, 2)
    wait_b(2)
    forward_two(b_copies)
    earlier_position(1)
    build_half(2, other)
    earlier_position(2)
    wait_a(3)
    prep_a(3)
    build_half(3, h)
    wait_b(3)
    build_half(3, other)
    earlier_position(3, last=True)
    log0, log1 = logs[0], logs[1]
    log_ref[0:PAIRS] = jnp.where(first, log0, pltpu.roll(log1, HALF, 1))
    log_ref[PAIRS:] = jnp.where(first, pltpu.roll(log0, HALF, 1), log1)

    write_log = pltpu.make_async_copy(log_ref, log_hbm, out_sem.at[2 * PAIRS])
    write_log.start()

    for copy in kv_out + q_out + kv_on + q_on:
        copy.wait_send()
    for copies in (a_copies, b_copies):
        for copy in copies(0, 0, 1, near):
            copy.wait_send()

    @pl.when(core == 0)
    def _():
        for copies in (a_copies, b_copies):
            for slot in range(1, 5):
                for copy in copies(slot, 0, 1, near):
                    copy.wait_send()

    for head in range(2 * PAIRS):
        write_out(head).wait()
    write_log.wait()


def on_device(block_table, a_query, b_query, a_key, b_key, a_value, b_value):
    rows = 2 * HALF
    heads = 2 * PAIRS
    hbm = pl.BlockSpec(memory_space=pltpu.HBM)
    dma = pltpu.SemaphoreType.DMA
    return pl.pallas_call(
        kernel,
        out_shape=(
            jax.ShapeDtypeStruct((heads, rows, DH), BF16),
            jax.ShapeDtypeStruct((heads, rows), F32),
        ),
        in_specs=[pl.BlockSpec(memory_space=pltpu.SMEM)] + [hbm] * 6,
        out_specs=(hbm, hbm),
        scratch_shapes=[
            pltpu.VMEM((2, HALF, 2 * DH), BF16),
            pltpu.VMEM((2, HALF // 2, RQ * DH), BF16),
            pltpu.VMEM((heads, rows, DH), BF16),
            pltpu.VMEM((heads, rows), F32),
            pltpu.VMEM((4, 8, 128), jnp.int32),
            pltpu.SMEM((4, 8, 128), jnp.int32),
            pltpu.VMEM((RQ, heads, rows), BF16),
            pltpu.VMEM((2, HALF, RQ * DH), BF16),
            pltpu.VMEM((4, 2, 2, HALF, 2 * DH), BF16),
            pltpu.VMEM((4, 4, heads, rows), BF16),
            pltpu.VMEM((2, RQ * DH, rows), F32),
            pltpu.VMEM((2, RQ, PAIRS, rows), F32),
            pltpu.VMEM((2, PAIRS, 2 * DH, rows), BF16),
            pltpu.VMEM((4, 2, HALF, 2 * DH), F32),
            pltpu.VMEM((4, 2, 2 * DH, HALF), F32),
            pltpu.VMEM((4, 2, HALF, 4 * PAIRS), BF16),
            pltpu.VMEM((4, 2, 2, heads, HALF), F32),
            pltpu.VMEM((4, 2, PAIRS, HALF, 2 * DH), BF16),
            pltpu.VMEM((4, 2, PAIRS, 2 * DH, HALF), BF16),
            pltpu.VMEM((2, PAIRS, DH, rows), F32),
            pltpu.VMEM((2, PAIRS, 1, rows), F32),
            pltpu.VMEM((2, PAIRS, 1, rows), F32),
            pltpu.VMEM((2, PAIRS, rows), F32),
            pltpu.VMEM((2 * DH, 2 * DH), BF16),
            pltpu.VMEM((PAIRS, 4 * PAIRS, 4 * DH), BF16),
            dma((heads + 1,)),
            dma((6,)),
            dma((4,)),
            dma((8,)),
            dma((8,)),
            dma((5,)),
            dma((3,)),
            dma((5,)),
            dma((3,)),
            dma((5,)),
            dma((3,)),
            dma((5,)),
            dma((3,)),
        ],
        compiler_params=pltpu.CompilerParams(
            collective_id=0, has_side_effects=True, vmem_limit_bytes=60 * 1024 * 1024
        ),
    )(block_table, a_query, b_query, a_key, b_key, a_value, b_value)


def solution(mesh):
    in_specs = (
        P("blk", None),
        P(None, "head", "blk"),
        P(("blk", "head"), None),
        P(None, "head", "blk"),
        P(("blk", "head"), None),
        P(None, "head", "blk"),
        P(("blk", "head"), None),
    )
    out_specs = (P("head", "blk", None), P("head", "blk"))
    return jax.shard_map(
        on_device, mesh=mesh, in_specs=in_specs, out_specs=out_specs, check_vma=False
    )
```

```python
import math

import jax
import jax.numpy as jnp
from jax import lax
from jax.experimental import pallas as pl
from jax.experimental.pallas import tpu as pltpu
from jax.sharding import PartitionSpec as P

HALF = 192
DH = 128
PAIRS = 8
RQ = 6
MESH = pl.DeviceIdType.MESH
F32 = jnp.float32
BF16 = jnp.bfloat16
SCALE = 0.5 / math.sqrt(DH)
MASKED = -1e30


def kernel(
    bt_in, aq_in, bq_in, ak_in, bk_in, av_in, bv_in,
    out_hbm, log_hbm,
    relay_kv, relay_q, out_ref, log_ref, bt, bts, aq, bq, bkv, akv,
    bqt, a2q, qbd, bkf, bvt, akt, avj, kb, vb,
    o_acc, m_acc, l_acc, logs, ident, spread,
    out_sem, local_sem, bts_sem, ex_send, ex_recv, a_send, a_recv, f_send, f_recv, t_send, t_recv, b_send, b_recv,
):
    e = lax.axis_index("blk")
    h = lax.axis_index("head")
    places = lax.axis_size("blk")
    other = 1 - h
    core = lax.rem(e, 2)
    lane = lax.broadcasted_iota(jnp.int32, (1, 2 * HALF), 1)
    first = lane < HALF

    def at(blk, head):
        return {"blk": lax.rem(blk + places, places), "head": head}

    across = e + places // 2
    chip = lax.rem(e // 2, places // 4)
    leaves = jnp.logical_and(chip == places // 4 - 1, core == 1)
    enters = jnp.logical_and(chip == 0, core == 0)

    barrier = pltpu.get_barrier_semaphore()

    def greet(target):
        pl.semaphore_signal(barrier, inc=1, device_id=target, device_id_type=MESH)

    greet(at(across, h))
    greet(at(across, other))
    greet(at(e - 1, h))

    @pl.when(enters)
    def _():
        greet(at(e - 1, other))

    locals_ = [
        pltpu.make_async_copy(src, dst, local_sem.at[i])
        for i, (src, dst) in enumerate(
            [
                (bk_in, bkv.at[0, h, 0]),
                (bv_in, bkv.at[0, h, 1]),
                (ak_in, akv.at[0, pl.ds(0, 2)]),
                (av_in, akv.at[0, pl.ds(2, 2)]),
                (bq_in, bq.at[h]),
                (aq_in, aq),
            ]
        )
    ]
    for copy in locals_:
        copy.start()
    side = (2 * DH, 2 * DH)
    ident[...] = (
        lax.broadcasted_iota(jnp.int32, side, 0) == lax.broadcasted_iota(jnp.int32, side, 1)
    ).astype(F32).astype(BF16)
    side = (4 * PAIRS, 4 * DH)
    source = lax.broadcasted_iota(jnp.int32, side, 0)
    wanted = lax.broadcasted_iota(jnp.int32, side, 1) // DH * PAIRS
    for p in range(PAIRS):
        spread[p] = (source == wanted + p).astype(F32).astype(BF16)
    own0, own1 = bt_in[0, 0], bt_in[0, 1]
    tlane = lax.broadcasted_iota(jnp.int32, (8, 128), 1)
    bt[0] = jnp.where(tlane == 0, own0, own1)
    pltpu.make_async_copy(bt.at[0], bts.at[0], bts_sem.at[0]).start()

    pl.semaphore_wait(barrier, 3 + leaves.astype(jnp.int32))

    def remote(src, dst, send, recv, target):
        return pltpu.make_async_remote_copy(
            src_ref=src, dst_ref=dst, send_sem=send, recv_sem=recv, device_id=target, device_id_type=MESH
        )

    ahead = at(e + 1, h)
    half = jnp.where(leaves, h, other)
    ahead_b = at(e + 1, 1 - half)

    def a_copies(s):
        return [
            remote(bkv.at[s, h], bkv.at[s + 1, h], a_send.at[s], a_recv.at[s], ahead),
            remote(akv.at[s], akv.at[s + 1], f_send.at[s], f_recv.at[s], ahead),
            remote(bt.at[s], bt.at[s + 1], t_send.at[s], t_recv.at[s], ahead),
        ]

    def b_copy(s):
        return remote(bkv.at[s, half], bkv.at[s + 1, half], b_send.at[s], b_recv.at[s], ahead_b)

    def start(copies):
        for copy in copies:
            copy.start()

    def send_a(s):
        start(a_copies(s))

        @pl.when(leaves)
        def _():
            b_copy(s).start()

    def send_b(s):
        @pl.when(jnp.logical_not(leaves))
        def _():
            b_copy(s).start()

    def fetch(s):
        return pltpu.make_async_copy(bt.at[s], bts.at[s], bts_sem.at[s])

    def wait_a(s):
        for copy in a_copies(s - 1):
            copy.wait_recv()
        fetch(s).start()
        if s < 3:
            send_a(s)

    def wait_b(s):
        remote(
            bkv.at[s - 1, other], bkv.at[s, other], b_send.at[s - 1], b_recv.at[s - 1], ahead
        ).wait_recv()
        if s < 3:
            send_b(s)

    same, cross = at(across, h), at(across, other)
    half_rows = HALF // 2

    def q_part(half, i):
        return bq.at[half, pl.ds(i * half_rows, half_rows)]

    def out_copy(i, src, dst, target):
        return remote(src, dst, ex_send.at[i], ex_recv.at[i], target)

    kv_out = [
        out_copy(0, bkv.at[0, h, 0], relay_kv.at[0], same),
        out_copy(1, bkv.at[0, h, 1], relay_kv.at[1], cross),
    ]
    q_out = [
        out_copy(2, q_part(h, 0), relay_q.at[0], same),
        out_copy(3, q_part(h, 1), relay_q.at[1], cross),
    ]
    kv_on = [
        out_copy(4, relay_kv.at[0], bkv.at[0, h, 0], cross),
        out_copy(5, relay_kv.at[1], bkv.at[0, other, 1], same),
    ]
    q_on = [
        out_copy(6, relay_q.at[0], q_part(h, 0), cross),
        out_copy(7, relay_q.at[1], q_part(other, 1), same),
    ]

    def pass_on(arrived, onward):
        for before, after in zip(arrived, onward):
            before.wait_recv()
            after.start()

    def wait_all(copies):
        for copy in copies:
            copy.wait_recv()

    for copy in locals_[:4]:
        copy.wait()
    start(kv_out)
    send_a(0)
    locals_[4].wait()
    start(q_out)
    locals_[5].wait()

    def scalars(s):
        fetch(s).wait()
        b0, b1 = bts[s, 0, 0], bts[s, 0, 1]
        return (b0 > b1).astype(jnp.int32), jnp.minimum(b0, b1)

    def dot(x, y):
        return jnp.dot(x, y, preferred_element_type=F32)

    def turn(y):
        n = y.shape[1]
        return lax.dot_general(ident[:n, :n], y, (((1,), (1,)), ((), ())), preferred_element_type=F32)

    def prep_a(s):
        keys = akv[s, 0:2].reshape(4 * PAIRS, 2 * HALF)
        keys_t = jnp.concatenate([turn(keys[:, i * DH : (i + 1) * DH]) for i in range(3)], axis=0)
        akt[s, 0] = keys_t[:HALF].astype(BF16)
        akt[s, 1] = keys_t[HALF:].astype(BF16)
        values = akv[s, 2:4].astype(F32)
        avj[s, 0] = values[:, :, :HALF]
        avj[s, 1] = values[:, :, HALF:]

    def prep_b(s, j):
        bkf[s, j] = bkv[s, j, 0].astype(F32)
        bvt[s, j] = turn(bkv[s, j, 1])

    def prep_q(j):
        for i in range(RQ // 2):
            b = bq[j, :, i * 2 * DH : (i + 1) * 2 * DH]
            bqt[j, i * 2 * DH : (i + 1) * 2 * DH] = turn(jnp.concatenate([b, b], axis=0))

    def prep_aq():
        x = aq[...].astype(F32)
        low, high = x[:, :PAIRS], x[:, PAIRS:]
        wide = first[None]

        def turned(y):
            return pltpu.roll(y.reshape(RQ * PAIRS, 2 * HALF), HALF, 1).reshape(y.shape)

        a2q[0] = jnp.where(wide, low, turned(high))
        a2q[1] = jnp.where(wide, turned(low), high)

    def build_q(j, p):
        total = a2q[j, 0, pl.ds(p, 1), :] * bqt[j, 0:DH, :]
        for r in range(1, RQ):
            total += a2q[j, r, pl.ds(p, 1), :] * bqt[j, r * DH : (r + 1) * DH, :]
        total = total * (1.0 / RQ)
        qbd[j, p, 0:DH] = jnp.where(first, total, 0.0).astype(BF16)
        qbd[j, p, DH : 2 * DH] = jnp.where(first, 0.0, total).astype(BF16)

    def build_kv(s, j, p):
        wide = dot(akt[s, j], spread[p])
        b0, b1 = bkf[s, j, :, 0:DH], bkf[s, j, :, DH : 2 * DH]
        ka = wide[:, 0:DH] * b0 + wide[:, 2 * DH : 3 * DH] * b1
        kb_ = wide[:, DH : 2 * DH] * b0 + wide[:, 3 * DH :] * b1
        c0, c1 = bvt[s, j, 0:DH], bvt[s, j, DH : 2 * DH]
        va = avj[s, j, 0, pl.ds(p, 1), :] * c0 + avj[s, j, 1, pl.ds(p, 1), :] * c1
        vb_ = avj[s, j, 0, pl.ds(p + PAIRS, 1), :] * c0 + avj[s, j, 1, pl.ds(p + PAIRS, 1), :] * c1
        kb[s, j, p, :, 0:DH] = ka.astype(BF16)
        kb[s, j, p, :, DH : 2 * DH] = kb_.astype(BF16)
        vb[s, j, p, 0:DH] = va.astype(BF16)
        vb[s, j, p, DH : 2 * DH] = vb_.astype(BF16)

    middle = lax.broadcasted_iota(jnp.int32, (1, DH), 1) < HALF - DH

    def weigh(scores, top, values):
        weights = jnp.exp((scores - top) * SCALE)
        total = jnp.sum(weights, axis=0, keepdims=True)
        rounded = weights.astype(BF16)
        both = dot(values, rounded[:, : 2 * DH])
        last = dot(values[DH:], rounded[:, 2 * DH :])
        out = jnp.concatenate(
            [both[:DH, :DH], jnp.where(middle, both[:DH, DH:], both[DH:, DH:]), last], axis=1
        )
        return total, out

    def highest(scores):
        return jnp.max(scores, axis=0, keepdims=True)

    def loop(body, width):
        each = PAIRS // width

        def step(p, carry):
            done = [body(p + i * each) for i in range(width)]
            for store in done:
                if store is not None:
                    store()
            return carry

        lax.fori_loop(0, each, step, 0)

    def build_half(s, j):
        prep_b(s, j)
        loop(lambda p: build_kv(s, j, p), 4)

    def put(which, p, state):
        m_acc[which, p], l_acc[which, p], o_acc[which, p] = state

    def get(which, p):
        return m_acc[which, p], l_acc[which, p], o_acc[which, p]

    def scores_of(s, j_keys, j_queries, p):
        return dot(kb[s, j_keys, p], qbd[j_queries, p])

    def own_blocks(p):
        shape = (HALF, 2 * HALF)
        row = lax.broadcasted_iota(jnp.int32, shape, 0)
        col = lax.broadcasted_iota(jnp.int32, shape, 1)
        seen = row <= jnp.where(col < HALF, col, col - HALF)
        low = jnp.where(seen, scores_of(0, jl0, jl0, p), MASKED)
        cross = scores_of(0, jl0, 1 - jl0, p)
        high = jnp.where(seen, scores_of(0, 1 - jl0, 1 - jl0, p), MASKED)
        v_low, v_high = vb[0, jl0, p], vb[0, 1 - jl0, p]
        return [(low, v_low)], [(cross, v_low), (high, v_high)]

    def choose(s):
        jls, lows = scalars(s)
        pick = (lows > low0).astype(jnp.int32)
        return s, jls, jls + pick - 2 * jls * pick, jl0 + pick - 2 * jl0 * pick, pick == 1

    def attend(offsets, last):
        chosen = [choose(s) for s in offsets]

        def body(p):
            if last:
                low_blocks, high_blocks = [], []
                m_low, l_low, o_low = get(0, p)
                m_high, l_high, o_high = get(1, p)
                low_tops, high_tops = [m_low], [m_high]
            else:
                low_blocks, high_blocks = own_blocks(p)
                low_tops, high_tops = [], []
            floating = []
            for s, jls, jk, jq, is_high in chosen:
                high_blocks.append((scores_of(s, jls, 1 - jl0, p), vb[s, jls, p]))
                scores = scores_of(s, jk, jq, p)
                floating.append((scores, vb[s, jk, p], is_high))
                top = highest(scores)
                high_tops.append(jnp.where(is_high, top, MASKED))
                low_tops.append(jnp.where(is_high, MASKED, top))
            low_tops += [highest(scores) for scores, _ in low_blocks]
            high_tops += [highest(scores) for scores, _ in high_blocks]
            low, high = low_tops[0], high_tops[0]
            for top in low_tops[1:]:
                low = jnp.maximum(low, top)
            for top in high_tops[1:]:
                high = jnp.maximum(high, top)
            low_parts = [weigh(scores, low, values) for scores, values in low_blocks]
            high_parts = [weigh(scores, high, values) for scores, values in high_blocks]
            for scores, values, is_high in floating:
                total, out = weigh(scores, jnp.where(is_high, high, low), values)
                high_parts.append((jnp.where(is_high, total, 0.0), jnp.where(is_high, out, 0.0)))
                low_parts.append((jnp.where(is_high, 0.0, total), jnp.where(is_high, 0.0, out)))
            if last:
                fade = jnp.exp((m_low - low) * SCALE)
                low_parts.append((l_low * fade, o_low * fade))
                fade = jnp.exp((m_high - high) * SCALE)
                high_parts.append((l_high * fade, o_high * fade))
            l_low, o_low = (sum(parts[1:], parts[0]) for parts in zip(*low_parts))
            l_high, o_high = (sum(parts[1:], parts[0]) for parts in zip(*high_parts))

            def store():
                if not last:
                    put(0, p, (low, l_low, o_low))
                    put(1, p, (high, l_high, o_high))
                    return
                rows_low = turned_rows((o_low * (0.5 / l_low)).astype(BF16))
                rows_high = turned_rows((o_high * (0.5 / l_high)).astype(BF16))
                log_low = low * SCALE + jnp.log(l_low)
                log_high = high * SCALE + jnp.log(l_high)
                for j in range(2):
                    is_low = jl0 == j
                    rows = jnp.where(is_low, rows_low, rows_high)
                    out_ref[p, j * HALF : (j + 1) * HALF, :] = rows[:HALF]
                    out_ref[p + PAIRS, j * HALF : (j + 1) * HALF, :] = rows[HALF:]
                    logs[j, pl.ds(p, 1), :] = jnp.where(is_low, log_low, log_high)
                for head in (p, p + PAIRS):
                    write_out(head).start()

            return store

        loop(body, 2)

    def turned_rows(x):
        parts = [turn(x[:, i * DH : (i + 1) * DH]) for i in range(3)]
        return jnp.concatenate(parts, axis=0).astype(BF16)

    def write_out(head):
        return pltpu.make_async_copy(out_ref.at[head], out_hbm.at[head], out_sem.at[head])

    jl0, low0 = scalars(0)
    prep_a(0)
    prep_aq()
    build_half(0, h)
    wait_a(1)
    pass_on(kv_out, kv_on)
    prep_q(h)
    loop(lambda p: build_q(h, p), 1)
    pass_on(q_out, q_on)
    prep_a(1)
    build_half(1, h)
    wait_a(2)
    wait_all(kv_on)
    send_b(0)
    build_half(0, other)
    wait_b(1)
    prep_a(2)
    build_half(2, h)
    build_half(1, other)
    wait_b(2)
    wait_all(q_on)
    prep_q(other)
    loop(lambda p: build_q(other, p), 1)
    build_half(2, other)
    attend([1], False)
    wait_a(3)
    prep_a(3)
    build_half(3, h)
    wait_b(3)
    build_half(3, other)
    attend([2, 3], True)
    log0, log1 = logs[0], logs[1]
    log_ref[0:PAIRS] = jnp.where(first, log0, pltpu.roll(log1, HALF, 1))
    log_ref[PAIRS:] = jnp.where(first, pltpu.roll(log0, HALF, 1), log1)

    write_log = pltpu.make_async_copy(log_ref, log_hbm, out_sem.at[2 * PAIRS])
    write_log.start()

    for copy in kv_out + q_out + kv_on + q_on:
        copy.wait_send()
    for s in range(3):
        for copy in a_copies(s) + [b_copy(s)]:
            copy.wait_send()

    for head in range(2 * PAIRS):
        write_out(head).wait()
    write_log.wait()


def on_device(block_table, a_query, b_query, a_key, b_key, a_value, b_value):
    rows = 2 * HALF
    heads = 2 * PAIRS
    hbm = pl.BlockSpec(memory_space=pltpu.HBM)
    dma = pltpu.SemaphoreType.DMA
    return pl.pallas_call(
        kernel,
        out_shape=(
            jax.ShapeDtypeStruct((heads, rows, DH), BF16),
            jax.ShapeDtypeStruct((heads, rows), F32),
        ),
        in_specs=[pl.BlockSpec(memory_space=pltpu.SMEM)] + [hbm] * 6,
        out_specs=(hbm, hbm),
        scratch_shapes=[
            pltpu.VMEM((2, HALF, 2 * DH), BF16),
            pltpu.VMEM((2, HALF // 2, RQ * DH), BF16),
            pltpu.VMEM((heads, rows, DH), BF16),
            pltpu.VMEM((heads, rows), F32),
            pltpu.VMEM((4, 8, 128), jnp.int32),
            pltpu.SMEM((4, 8, 128), jnp.int32),
            pltpu.VMEM((RQ, heads, rows), BF16),
            pltpu.VMEM((2, HALF, RQ * DH), BF16),
            pltpu.VMEM((4, 2, 2, HALF, 2 * DH), BF16),
            pltpu.VMEM((4, 4, heads, rows), BF16),
            pltpu.VMEM((2, RQ * DH, rows), F32),
            pltpu.VMEM((2, RQ, PAIRS, rows), F32),
            pltpu.VMEM((2, PAIRS, 2 * DH, rows), BF16),
            pltpu.VMEM((4, 2, HALF, 2 * DH), F32),
            pltpu.VMEM((4, 2, 2 * DH, HALF), F32),
            pltpu.VMEM((4, 2, HALF, 4 * PAIRS), BF16),
            pltpu.VMEM((4, 2, 2, heads, HALF), F32),
            pltpu.VMEM((4, 2, PAIRS, HALF, 2 * DH), BF16),
            pltpu.VMEM((4, 2, PAIRS, 2 * DH, HALF), BF16),
            pltpu.VMEM((2, PAIRS, DH, rows), F32),
            pltpu.VMEM((2, PAIRS, 1, rows), F32),
            pltpu.VMEM((2, PAIRS, 1, rows), F32),
            pltpu.VMEM((2, PAIRS, rows), F32),
            pltpu.VMEM((2 * DH, 2 * DH), BF16),
            pltpu.VMEM((PAIRS, 4 * PAIRS, 4 * DH), BF16),
            dma((heads + 1,)),
            dma((6,)),
            dma((4,)),
            dma((8,)),
            dma((8,)),
            dma((3,)),
            dma((3,)),
            dma((3,)),
            dma((3,)),
            dma((3,)),
            dma((3,)),
            dma((3,)),
            dma((3,)),
        ],
        compiler_params=pltpu.CompilerParams(
            collective_id=0, has_side_effects=True, vmem_limit_bytes=60 * 1024 * 1024
        ),
    )(block_table, a_query, b_query, a_key, b_key, a_value, b_value)


def solution(mesh):
    in_specs = (
        P("blk", None),
        P(None, "head", "blk"),
        P(("blk", "head"), None),
        P(None, "head", "blk"),
        P(("blk", "head"), None),
        P(None, "head", "blk"),
        P(("blk", "head"), None),
    )
    out_specs = (P("head", "blk", None), P("head", "blk"))
    return jax.shard_map(
        on_device, mesh=mesh, in_specs=in_specs, out_specs=out_specs, check_vma=False
    )
```

```python
import math

import jax
import jax.numpy as jnp
from jax import lax
from jax.experimental import pallas as pl
from jax.experimental.pallas import tpu as pltpu
from jax.sharding import PartitionSpec as P

HALF = 192
DH = 128
PAIRS = 8
RQ = 6
MESH = pl.DeviceIdType.MESH
F32 = jnp.float32
BF16 = jnp.bfloat16
SCALE = 0.5 / math.sqrt(DH)
MASKED = -1e30


def kernel(
    bt_in, aq_in, bq_in, ak_in, bk_in, av_in, bv_in,
    out_hbm, log_hbm,
    relay_kv, relay_q, out_ref, log_ref, bt, bts, aq, bq, bkv, akv,
    bqt, a2q, qbd, bkf, bvt, akt, avj, kb, vb,
    o_acc, m_acc, l_acc, logs, ident, spread,
    out_sem, local_sem, bts_sem, ex_send, ex_recv, a_send, a_recv, f_send, f_recv, t_send, t_recv, b_send, b_recv,
):
    e = lax.axis_index("blk")
    h = lax.axis_index("head")
    places = lax.axis_size("blk")
    other = 1 - h
    core = lax.rem(e, 2)
    lane = lax.broadcasted_iota(jnp.int32, (1, 2 * HALF), 1)
    first = lane < HALF

    def at(blk, head):
        return {"blk": lax.rem(blk + places, places), "head": head}

    across = e + places // 2
    chip = lax.rem(e // 2, places // 4)
    leaves = jnp.logical_and(chip == places // 4 - 1, core == 1)
    enters = jnp.logical_and(chip == 0, core == 0)

    barrier = pltpu.get_barrier_semaphore()

    def greet(target):
        pl.semaphore_signal(barrier, inc=1, device_id=target, device_id_type=MESH)

    greet(at(across, h))
    greet(at(across, other))
    greet(at(e - 1, h))

    @pl.when(enters)
    def _():
        greet(at(e - 1, other))

    locals_ = [
        pltpu.make_async_copy(src, dst, local_sem.at[i])
        for i, (src, dst) in enumerate(
            [
                (bk_in, bkv.at[0, h, 0]),
                (bv_in, bkv.at[0, h, 1]),
                (ak_in, akv.at[0, pl.ds(0, 2)]),
                (av_in, akv.at[0, pl.ds(2, 2)]),
                (bq_in, bq.at[h]),
                (aq_in, aq),
            ]
        )
    ]
    for copy in locals_:
        copy.start()
    side = (2 * DH, 2 * DH)
    ident[...] = (
        lax.broadcasted_iota(jnp.int32, side, 0) == lax.broadcasted_iota(jnp.int32, side, 1)
    ).astype(F32).astype(BF16)
    side = (4 * PAIRS, 4 * DH)
    source = lax.broadcasted_iota(jnp.int32, side, 0)
    wanted = lax.broadcasted_iota(jnp.int32, side, 1) // DH * PAIRS
    for p in range(PAIRS):
        spread[p] = (source == wanted + p).astype(F32).astype(BF16)
    own0, own1 = bt_in[0, 0], bt_in[0, 1]
    tlane = lax.broadcasted_iota(jnp.int32, (8, 128), 1)
    bt[0] = jnp.where(tlane == 0, own0, own1)
    pltpu.make_async_copy(bt.at[0], bts.at[0], bts_sem.at[0]).start()

    pl.semaphore_wait(barrier, 3 + leaves.astype(jnp.int32))

    def remote(src, dst, send, recv, target):
        return pltpu.make_async_remote_copy(
            src_ref=src, dst_ref=dst, send_sem=send, recv_sem=recv, device_id=target, device_id_type=MESH
        )

    ahead = at(e + 1, h)
    half = jnp.where(leaves, h, other)
    ahead_b = at(e + 1, 1 - half)

    def a_copies(s):
        return [
            remote(bkv.at[s, h], bkv.at[s + 1, h], a_send.at[s], a_recv.at[s], ahead),
            remote(akv.at[s], akv.at[s + 1], f_send.at[s], f_recv.at[s], ahead),
            remote(bt.at[s], bt.at[s + 1], t_send.at[s], t_recv.at[s], ahead),
        ]

    def b_copy(s):
        return remote(bkv.at[s, half], bkv.at[s + 1, half], b_send.at[s], b_recv.at[s], ahead_b)

    def start(copies):
        for copy in copies:
            copy.start()

    def send_a(s):
        start(a_copies(s))

        @pl.when(leaves)
        def _():
            b_copy(s).start()

    def send_b(s):
        @pl.when(jnp.logical_not(leaves))
        def _():
            b_copy(s).start()

    def fetch(s):
        return pltpu.make_async_copy(bt.at[s], bts.at[s], bts_sem.at[s])

    def wait_a(s):
        for copy in a_copies(s - 1):
            copy.wait_recv()
        fetch(s).start()
        if s < 3:
            send_a(s)

    def wait_b(s):
        remote(
            bkv.at[s - 1, other], bkv.at[s, other], b_send.at[s - 1], b_recv.at[s - 1], ahead
        ).wait_recv()
        if s < 3:
            send_b(s)

    same, cross = at(across, h), at(across, other)
    half_rows = HALF // 2

    def q_part(half, i):
        return bq.at[half, pl.ds(i * half_rows, half_rows)]

    def out_copy(i, src, dst, target):
        return remote(src, dst, ex_send.at[i], ex_recv.at[i], target)

    kv_out = [
        out_copy(0, bkv.at[0, h, 0], relay_kv.at[0], same),
        out_copy(1, bkv.at[0, h, 1], relay_kv.at[1], cross),
    ]
    q_out = [
        out_copy(2, q_part(h, 0), relay_q.at[0], same),
        out_copy(3, q_part(h, 1), relay_q.at[1], cross),
    ]
    kv_on = [
        out_copy(4, relay_kv.at[0], bkv.at[0, h, 0], cross),
        out_copy(5, relay_kv.at[1], bkv.at[0, other, 1], same),
    ]
    q_on = [
        out_copy(6, relay_q.at[0], q_part(h, 0), cross),
        out_copy(7, relay_q.at[1], q_part(other, 1), same),
    ]

    def pass_on(arrived, onward):
        for before, after in zip(arrived, onward):
            before.wait_recv()
            after.start()

    def wait_all(copies):
        for copy in copies:
            copy.wait_recv()

    for copy in locals_[:4]:
        copy.wait()
    start(kv_out)
    send_a(0)
    locals_[4].wait()
    start(q_out)
    locals_[5].wait()

    def scalars(s):
        fetch(s).wait()
        b0, b1 = bts[s, 0, 0], bts[s, 0, 1]
        return (b0 > b1).astype(jnp.int32), jnp.minimum(b0, b1)

    def dot(x, y):
        return jnp.dot(x, y, preferred_element_type=F32)

    def turn(y):
        n = y.shape[1]
        return lax.dot_general(ident[:n, :n], y, (((1,), (1,)), ((), ())), preferred_element_type=F32)

    def prep_a(s):
        keys = akv[s, 0:2].reshape(4 * PAIRS, 2 * HALF)
        keys_t = jnp.concatenate([turn(keys[:, i * DH : (i + 1) * DH]) for i in range(3)], axis=0)
        akt[s, 0] = keys_t[:HALF].astype(BF16)
        akt[s, 1] = keys_t[HALF:].astype(BF16)
        values = akv[s, 2:4].astype(F32)
        avj[s, 0] = values[:, :, :HALF]
        avj[s, 1] = values[:, :, HALF:]

    def prep_b(s, j):
        bkf[s, j] = bkv[s, j, 0].astype(F32)
        bvt[s, j] = turn(bkv[s, j, 1])

    def prep_q(j):
        for i in range(RQ // 2):
            b = bq[j, :, i * 2 * DH : (i + 1) * 2 * DH]
            bqt[j, i * 2 * DH : (i + 1) * 2 * DH] = turn(jnp.concatenate([b, b], axis=0))

    def prep_aq():
        x = aq[...].astype(F32)
        low, high = x[:, :PAIRS], x[:, PAIRS:]
        wide = first[None]

        def turned(y):
            return pltpu.roll(y.reshape(RQ * PAIRS, 2 * HALF), HALF, 1).reshape(y.shape)

        a2q[0] = jnp.where(wide, low, turned(high))
        a2q[1] = jnp.where(wide, turned(low), high)

    def build_q(j, p):
        total = a2q[j, 0, pl.ds(p, 1), :] * bqt[j, 0:DH, :]
        for r in range(1, RQ):
            total += a2q[j, r, pl.ds(p, 1), :] * bqt[j, r * DH : (r + 1) * DH, :]
        total = total * (1.0 / RQ)
        qbd[j, p, 0:DH] = jnp.where(first, total, 0.0).astype(BF16)
        qbd[j, p, DH : 2 * DH] = jnp.where(first, 0.0, total).astype(BF16)

    def build_kv(s, j, p):
        wide = dot(akt[s, j], spread[p])
        b0, b1 = bkf[s, j, :, 0:DH], bkf[s, j, :, DH : 2 * DH]
        ka = wide[:, 0:DH] * b0 + wide[:, 2 * DH : 3 * DH] * b1
        kb_ = wide[:, DH : 2 * DH] * b0 + wide[:, 3 * DH :] * b1
        c0, c1 = bvt[s, j, 0:DH], bvt[s, j, DH : 2 * DH]
        va = avj[s, j, 0, pl.ds(p, 1), :] * c0 + avj[s, j, 1, pl.ds(p, 1), :] * c1
        vb_ = avj[s, j, 0, pl.ds(p + PAIRS, 1), :] * c0 + avj[s, j, 1, pl.ds(p + PAIRS, 1), :] * c1
        kb[s, j, p, :, 0:DH] = ka.astype(BF16)
        kb[s, j, p, :, DH : 2 * DH] = kb_.astype(BF16)
        vb[s, j, p, 0:DH] = va.astype(BF16)
        vb[s, j, p, DH : 2 * DH] = vb_.astype(BF16)

    middle = lax.broadcasted_iota(jnp.int32, (1, DH), 1) < HALF - DH

    def weigh(scores, top, values):
        weights = jnp.exp((scores - top) * SCALE)
        total = jnp.sum(weights, axis=0, keepdims=True)
        rounded = weights.astype(BF16)
        both = dot(values, rounded[:, : 2 * DH])
        last = dot(values[DH:], rounded[:, 2 * DH :])
        out = jnp.concatenate(
            [both[:DH, :DH], jnp.where(middle, both[:DH, DH:], both[DH:, DH:]), last], axis=1
        )
        return total, out

    def highest(scores):
        return jnp.max(scores, axis=0, keepdims=True)

    def loop(body, width):
        each = PAIRS // width

        def step(p, carry):
            done = [body(p + i * each) for i in range(width)]
            for store in done:
                if store is not None:
                    store()
            return carry

        lax.fori_loop(0, each, step, 0)

    def build_half(s, j):
        prep_b(s, j)
        loop(lambda p: build_kv(s, j, p), 4)

    def put(which, p, state):
        m_acc[which, p], l_acc[which, p], o_acc[which, p] = state

    def get(which, p):
        return m_acc[which, p], l_acc[which, p], o_acc[which, p]

    def scores_of(s, j_keys, j_queries, p):
        return dot(kb[s, j_keys, p], qbd[j_queries, p])

    def own_blocks(p):
        shape = (HALF, 2 * HALF)
        row = lax.broadcasted_iota(jnp.int32, shape, 0)
        col = lax.broadcasted_iota(jnp.int32, shape, 1)
        seen = row <= jnp.where(col < HALF, col, col - HALF)
        low = jnp.where(seen, scores_of(0, jl0, jl0, p), MASKED)
        cross = scores_of(0, jl0, 1 - jl0, p)
        high = jnp.where(seen, scores_of(0, 1 - jl0, 1 - jl0, p), MASKED)
        v_low, v_high = vb[0, jl0, p], vb[0, 1 - jl0, p]
        return [(low, v_low)], [(cross, v_low), (high, v_high)]

    def choose(s):
        jls, lows = scalars(s)
        pick = (lows > low0).astype(jnp.int32)
        return s, jls, jls + pick - 2 * jls * pick, jl0 + pick - 2 * jl0 * pick, pick == 1

    def attend(offsets, width, last=False):
        chosen = [choose(s) for s in offsets]

        def body(p):
            if offsets:
                low_blocks, high_blocks = [], []
                m_low, l_low, o_low = get(0, p)
                m_high, l_high, o_high = get(1, p)
                low_tops, high_tops = [m_low], [m_high]
            else:
                low_blocks, high_blocks = own_blocks(p)
                low_tops, high_tops = [], []
            floating = []
            for s, jls, jk, jq, is_high in chosen:
                high_blocks.append((scores_of(s, jls, 1 - jl0, p), vb[s, jls, p]))
                scores = scores_of(s, jk, jq, p)
                floating.append((scores, vb[s, jk, p], is_high))
                top = highest(scores)
                high_tops.append(jnp.where(is_high, top, MASKED))
                low_tops.append(jnp.where(is_high, MASKED, top))
            low_tops += [highest(scores) for scores, _ in low_blocks]
            high_tops += [highest(scores) for scores, _ in high_blocks]
            low, high = low_tops[0], high_tops[0]
            for top in low_tops[1:]:
                low = jnp.maximum(low, top)
            for top in high_tops[1:]:
                high = jnp.maximum(high, top)
            low_parts = [weigh(scores, low, values) for scores, values in low_blocks]
            high_parts = [weigh(scores, high, values) for scores, values in high_blocks]
            for scores, values, is_high in floating:
                total, out = weigh(scores, jnp.where(is_high, high, low), values)
                high_parts.append((jnp.where(is_high, total, 0.0), jnp.where(is_high, out, 0.0)))
                low_parts.append((jnp.where(is_high, 0.0, total), jnp.where(is_high, 0.0, out)))
            if offsets:
                fade = jnp.exp((m_low - low) * SCALE)
                low_parts.append((l_low * fade, o_low * fade))
                fade = jnp.exp((m_high - high) * SCALE)
                high_parts.append((l_high * fade, o_high * fade))
            l_low, o_low = (sum(parts[1:], parts[0]) for parts in zip(*low_parts))
            l_high, o_high = (sum(parts[1:], parts[0]) for parts in zip(*high_parts))

            def store():
                if not last:
                    put(0, p, (low, l_low, o_low))
                    put(1, p, (high, l_high, o_high))
                    return
                rows_low = turned_rows((o_low * (0.5 / l_low)).astype(BF16))
                rows_high = turned_rows((o_high * (0.5 / l_high)).astype(BF16))
                log_low = low * SCALE + jnp.log(l_low)
                log_high = high * SCALE + jnp.log(l_high)
                for j in range(2):
                    is_low = jl0 == j
                    rows = jnp.where(is_low, rows_low, rows_high)
                    out_ref[p, j * HALF : (j + 1) * HALF, :] = rows[:HALF]
                    out_ref[p + PAIRS, j * HALF : (j + 1) * HALF, :] = rows[HALF:]
                    logs[j, pl.ds(p, 1), :] = jnp.where(is_low, log_low, log_high)
                for head in (p, p + PAIRS):
                    write_out(head).start()

            return store

        loop(body, width)

    def turned_rows(x):
        parts = [turn(x[:, i * DH : (i + 1) * DH]) for i in range(3)]
        return jnp.concatenate(parts, axis=0).astype(BF16)

    def write_out(head):
        return pltpu.make_async_copy(out_ref.at[head], out_hbm.at[head], out_sem.at[head])

    jl0, low0 = scalars(0)
    prep_a(0)
    prep_aq()
    build_half(0, h)
    pass_on(kv_out, kv_on)
    prep_q(h)
    loop(lambda p: build_q(h, p), 1)
    pass_on(q_out, q_on)
    wait_all(kv_on)
    send_b(0)
    build_half(0, other)
    wait_a(1)
    wait_all(q_on)
    prep_q(other)
    loop(lambda p: build_q(other, p), 1)
    prep_a(1)
    build_half(1, h)
    attend([], 2)
    wait_a(2)
    wait_b(1)
    build_half(1, other)
    prep_a(2)
    build_half(2, h)
    wait_b(2)
    attend([1], 4)
    build_half(2, other)
    wait_a(3)
    prep_a(3)
    build_half(3, h)
    wait_b(3)
    build_half(3, other)
    attend([2, 3], 2, last=True)
    log0, log1 = logs[0], logs[1]
    log_ref[0:PAIRS] = jnp.where(first, log0, pltpu.roll(log1, HALF, 1))
    log_ref[PAIRS:] = jnp.where(first, pltpu.roll(log0, HALF, 1), log1)

    write_log = pltpu.make_async_copy(log_ref, log_hbm, out_sem.at[2 * PAIRS])
    write_log.start()

    for copy in kv_out + q_out + kv_on + q_on:
        copy.wait_send()
    for s in range(3):
        for copy in a_copies(s) + [b_copy(s)]:
            copy.wait_send()

    for head in range(2 * PAIRS):
        write_out(head).wait()
    write_log.wait()


def on_device(block_table, a_query, b_query, a_key, b_key, a_value, b_value):
    rows = 2 * HALF
    heads = 2 * PAIRS
    hbm = pl.BlockSpec(memory_space=pltpu.HBM)
    dma = pltpu.SemaphoreType.DMA
    return pl.pallas_call(
        kernel,
        out_shape=(
            jax.ShapeDtypeStruct((heads, rows, DH), BF16),
            jax.ShapeDtypeStruct((heads, rows), F32),
        ),
        in_specs=[pl.BlockSpec(memory_space=pltpu.SMEM)] + [hbm] * 6,
        out_specs=(hbm, hbm),
        scratch_shapes=[
            pltpu.VMEM((2, HALF, 2 * DH), BF16),
            pltpu.VMEM((2, HALF // 2, RQ * DH), BF16),
            pltpu.VMEM((heads, rows, DH), BF16),
            pltpu.VMEM((heads, rows), F32),
            pltpu.VMEM((4, 8, 128), jnp.int32),
            pltpu.SMEM((4, 8, 128), jnp.int32),
            pltpu.VMEM((RQ, heads, rows), BF16),
            pltpu.VMEM((2, HALF, RQ * DH), BF16),
            pltpu.VMEM((4, 2, 2, HALF, 2 * DH), BF16),
            pltpu.VMEM((4, 4, heads, rows), BF16),
            pltpu.VMEM((2, RQ * DH, rows), F32),
            pltpu.VMEM((2, RQ, PAIRS, rows), F32),
            pltpu.VMEM((2, PAIRS, 2 * DH, rows), BF16),
            pltpu.VMEM((4, 2, HALF, 2 * DH), F32),
            pltpu.VMEM((4, 2, 2 * DH, HALF), F32),
            pltpu.VMEM((4, 2, HALF, 4 * PAIRS), BF16),
            pltpu.VMEM((4, 2, 2, heads, HALF), F32),
            pltpu.VMEM((4, 2, PAIRS, HALF, 2 * DH), BF16),
            pltpu.VMEM((4, 2, PAIRS, 2 * DH, HALF), BF16),
            pltpu.VMEM((2, PAIRS, DH, rows), F32),
            pltpu.VMEM((2, PAIRS, 1, rows), F32),
            pltpu.VMEM((2, PAIRS, 1, rows), F32),
            pltpu.VMEM((2, PAIRS, rows), F32),
            pltpu.VMEM((2 * DH, 2 * DH), BF16),
            pltpu.VMEM((PAIRS, 4 * PAIRS, 4 * DH), BF16),
            dma((heads + 1,)),
            dma((6,)),
            dma((4,)),
            dma((8,)),
            dma((8,)),
            dma((3,)),
            dma((3,)),
            dma((3,)),
            dma((3,)),
            dma((3,)),
            dma((3,)),
            dma((3,)),
            dma((3,)),
        ],
        compiler_params=pltpu.CompilerParams(
            collective_id=0, has_side_effects=True, vmem_limit_bytes=60 * 1024 * 1024
        ),
    )(block_table, a_query, b_query, a_key, b_key, a_value, b_value)


def solution(mesh):
    in_specs = (
        P("blk", None),
        P(None, "head", "blk"),
        P(("blk", "head"), None),
        P(None, "head", "blk"),
        P(("blk", "head"), None),
        P(None, "head", "blk"),
        P(("blk", "head"), None),
    )
    out_specs = (P("head", "blk", None), P("head", "blk"))
    return jax.shard_map(
        on_device, mesh=mesh, in_specs=in_specs, out_specs=out_specs, check_vma=False
    )
```

```python
import math

import jax
import jax.numpy as jnp
from jax import lax
from jax.experimental import pallas as pl
from jax.experimental.pallas import tpu as pltpu
from jax.sharding import PartitionSpec as P

HALF = 192
DH = 128
PAIRS = 8
RQ = 6
MESH = pl.DeviceIdType.MESH
F32 = jnp.float32
BF16 = jnp.bfloat16
SCALE = 0.5 / math.sqrt(DH)
MASKED = -1e30


def kernel(
    bt_in, aq_in, bq_in, ak_in, bk_in, av_in, bv_in,
    out_hbm, log_hbm,
    relay_kv, relay_q, out_ref, log_ref, bt, bts, aq, bq, bkv, akv,
    bqt, a2q, qbd, bkf, bvt, akt, avj, kb0, kb1, kb2, kb3, vb0, vb1, vb2, vb3,
    o_acc, m_acc, l_acc, logs, ident, spread,
    out_sem, local_sem, bts_sem, ex_send, ex_recv, a_send, a_recv, f_send, f_recv, t_send, t_recv, b_send, b_recv,
):
    kb, vb = (kb0, kb1, kb2, kb3), (vb0, vb1, vb2, vb3)
    e = lax.axis_index("blk")
    h = lax.axis_index("head")
    places = lax.axis_size("blk")
    other = 1 - h
    core = lax.rem(e, 2)
    lane = lax.broadcasted_iota(jnp.int32, (1, 2 * HALF), 1)
    first = lane < HALF

    def at(blk, head):
        return {"blk": lax.rem(blk + places, places), "head": head}

    across = e + places // 2
    chip = lax.rem(e // 2, places // 4)
    leaves = jnp.logical_and(chip == places // 4 - 1, core == 1)
    enters = jnp.logical_and(chip == 0, core == 0)

    barrier = pltpu.get_barrier_semaphore()

    def greet(target):
        pl.semaphore_signal(barrier, inc=1, device_id=target, device_id_type=MESH)

    greet(at(across, h))
    greet(at(across, other))
    greet(at(e - 1, h))

    @pl.when(enters)
    def _():
        greet(at(e - 1, other))

    locals_ = [
        pltpu.make_async_copy(src, dst, local_sem.at[i])
        for i, (src, dst) in enumerate(
            [
                (bk_in, bkv.at[0, h, 0]),
                (bv_in, bkv.at[0, h, 1]),
                (ak_in, akv.at[0, pl.ds(0, 2)]),
                (av_in, akv.at[0, pl.ds(2, 2)]),
                (bq_in, bq.at[h]),
                (aq_in, aq),
            ]
        )
    ]
    for copy in locals_:
        copy.start()
    side = (2 * DH, 2 * DH)
    ident[...] = (
        lax.broadcasted_iota(jnp.int32, side, 0) == lax.broadcasted_iota(jnp.int32, side, 1)
    ).astype(F32).astype(BF16)
    side = (4 * PAIRS, 4 * DH)
    source = lax.broadcasted_iota(jnp.int32, side, 0)
    wanted = lax.broadcasted_iota(jnp.int32, side, 1) // DH * PAIRS
    for p in range(PAIRS):
        spread[p] = (source == wanted + p).astype(F32).astype(BF16)
    own0, own1 = bt_in[0, 0], bt_in[0, 1]
    tlane = lax.broadcasted_iota(jnp.int32, (8, 128), 1)
    bt[0] = jnp.where(tlane == 0, own0, own1)
    pltpu.make_async_copy(bt.at[0], bts.at[0], bts_sem.at[0]).start()

    pl.semaphore_wait(barrier, 3 + leaves.astype(jnp.int32))

    def remote(src, dst, send, recv, target):
        return pltpu.make_async_remote_copy(
            src_ref=src, dst_ref=dst, send_sem=send, recv_sem=recv, device_id=target, device_id_type=MESH
        )

    ahead = at(e + 1, h)
    half = jnp.where(leaves, h, other)
    ahead_b = at(e + 1, 1 - half)

    def a_copies(s):
        return [
            remote(bkv.at[s, h], bkv.at[s + 1, h], a_send.at[s], a_recv.at[s], ahead),
            remote(akv.at[s], akv.at[s + 1], f_send.at[s], f_recv.at[s], ahead),
            remote(bt.at[s], bt.at[s + 1], t_send.at[s], t_recv.at[s], ahead),
        ]

    def b_copy(s):
        return remote(bkv.at[s, half], bkv.at[s + 1, half], b_send.at[s], b_recv.at[s], ahead_b)

    def start(copies):
        for copy in copies:
            copy.start()

    def send_a(s):
        start(a_copies(s))

        @pl.when(leaves)
        def _():
            b_copy(s).start()

    def send_b(s):
        @pl.when(jnp.logical_not(leaves))
        def _():
            b_copy(s).start()

    def fetch(s):
        return pltpu.make_async_copy(bt.at[s], bts.at[s], bts_sem.at[s])

    def wait_a(s):
        for copy in a_copies(s - 1):
            copy.wait_recv()
        fetch(s).start()
        if s < 3:
            send_a(s)

    def wait_b(s):
        remote(
            bkv.at[s - 1, other], bkv.at[s, other], b_send.at[s - 1], b_recv.at[s - 1], ahead
        ).wait_recv()
        if s < 3:
            send_b(s)

    same, cross = at(across, h), at(across, other)
    half_rows = HALF // 2

    def q_part(half, i):
        return bq.at[half, pl.ds(i * half_rows, half_rows)]

    def out_copy(i, src, dst, target):
        return remote(src, dst, ex_send.at[i], ex_recv.at[i], target)

    kv_out = [
        out_copy(0, bkv.at[0, h, 0], relay_kv.at[0], same),
        out_copy(1, bkv.at[0, h, 1], relay_kv.at[1], cross),
    ]
    q_out = [
        out_copy(2, q_part(h, 0), relay_q.at[0], same),
        out_copy(3, q_part(h, 1), relay_q.at[1], cross),
    ]
    kv_on = [
        out_copy(4, relay_kv.at[0], bkv.at[0, h, 0], cross),
        out_copy(5, relay_kv.at[1], bkv.at[0, other, 1], same),
    ]
    q_on = [
        out_copy(6, relay_q.at[0], q_part(h, 0), cross),
        out_copy(7, relay_q.at[1], q_part(other, 1), same),
    ]

    def pass_on(arrived, onward):
        for before, after in zip(arrived, onward):
            before.wait_recv()
            after.start()

    def wait_all(copies):
        for copy in copies:
            copy.wait_recv()

    for copy in locals_[:4]:
        copy.wait()
    start(kv_out)
    send_a(0)
    locals_[4].wait()
    start(q_out)
    locals_[5].wait()

    def scalars(s):
        fetch(s).wait()
        b0, b1 = bts[s, 0, 0], bts[s, 0, 1]
        return (b0 > b1).astype(jnp.int32), jnp.minimum(b0, b1)

    def dot(x, y):
        return jnp.dot(x, y, preferred_element_type=F32)

    def turn(y):
        n = y.shape[1]
        return lax.dot_general(ident[:n, :n], y, (((1,), (1,)), ((), ())), preferred_element_type=F32)

    def prep_a(s):
        keys = akv[s, 0:2].reshape(4 * PAIRS, 2 * HALF)
        keys_t = jnp.concatenate([turn(keys[:, i * DH : (i + 1) * DH]) for i in range(3)], axis=0)
        akt[s, 0] = keys_t[:HALF].astype(BF16)
        akt[s, 1] = keys_t[HALF:].astype(BF16)
        values = akv[s, 2:4].astype(F32)
        avj[s, 0] = values[:, :, :HALF]
        avj[s, 1] = values[:, :, HALF:]

    def prep_b(s, j):
        bkf[s, j] = bkv[s, j, 0].astype(F32)
        bvt[s, j] = turn(bkv[s, j, 1])

    def prep_q(j):
        for i in range(RQ // 2):
            b = bq[j, :, i * 2 * DH : (i + 1) * 2 * DH]
            bqt[j, i * 2 * DH : (i + 1) * 2 * DH] = turn(jnp.concatenate([b, b], axis=0))

    def prep_aq():
        x = aq[...].astype(F32)
        low, high = x[:, :PAIRS], x[:, PAIRS:]
        wide = first[None]

        def turned(y):
            return pltpu.roll(y.reshape(RQ * PAIRS, 2 * HALF), HALF, 1).reshape(y.shape)

        a2q[0] = jnp.where(wide, low, turned(high))
        a2q[1] = jnp.where(wide, turned(low), high)

    def build_q(j, p):
        total = a2q[j, 0, pl.ds(p, 1), :] * bqt[j, 0:DH, :]
        for r in range(1, RQ):
            total += a2q[j, r, pl.ds(p, 1), :] * bqt[j, r * DH : (r + 1) * DH, :]
        total = total * (1.0 / RQ)
        qbd[j, p, 0:DH] = jnp.where(first, total, 0.0).astype(BF16)
        qbd[j, p, DH : 2 * DH] = jnp.where(first, 0.0, total).astype(BF16)

    def build_kv(s, j, p):
        wide = dot(akt[s, j], spread[p])
        b0, b1 = bkf[s, j, :, 0:DH], bkf[s, j, :, DH : 2 * DH]
        ka = wide[:, 0:DH] * b0 + wide[:, 2 * DH : 3 * DH] * b1
        kb_ = wide[:, DH : 2 * DH] * b0 + wide[:, 3 * DH :] * b1
        c0, c1 = bvt[s, j, 0:DH], bvt[s, j, DH : 2 * DH]
        va = avj[s, j, 0, pl.ds(p, 1), :] * c0 + avj[s, j, 1, pl.ds(p, 1), :] * c1
        vb_ = avj[s, j, 0, pl.ds(p + PAIRS, 1), :] * c0 + avj[s, j, 1, pl.ds(p + PAIRS, 1), :] * c1
        kb[s][j, p, :, 0:DH] = ka.astype(BF16)
        kb[s][j, p, :, DH : 2 * DH] = kb_.astype(BF16)
        vb[s][j, p, 0:DH] = va.astype(BF16)
        vb[s][j, p, DH : 2 * DH] = vb_.astype(BF16)

    middle = lax.broadcasted_iota(jnp.int32, (1, DH), 1) < HALF - DH

    def weigh(scores, top, values):
        weights = jnp.exp((scores - top) * SCALE)
        total = jnp.sum(weights, axis=0, keepdims=True)
        rounded = weights.astype(BF16)
        both = dot(values, rounded[:, : 2 * DH])
        last = dot(values[DH:], rounded[:, 2 * DH :])
        out = jnp.concatenate(
            [both[:DH, :DH], jnp.where(middle, both[:DH, DH:], both[DH:, DH:]), last], axis=1
        )
        return total, out

    def highest(scores):
        return jnp.max(scores, axis=0, keepdims=True)

    def loop(body, width):
        each = PAIRS // width

        def step(p, carry):
            done = [body(p + i * each) for i in range(width)]
            for store in done:
                if store is not None:
                    store()
            return carry

        lax.fori_loop(0, each, step, 0)

    def build_all(*builds):
        def body(p):
            for build in builds:
                build(p)

        loop(body, 4 if len(builds) == 1 else 2)

    def kv(s, j):
        return lambda p: build_kv(s, j, p)

    def q(j):
        return lambda p: build_q(j, p)

    def put(which, p, state):
        m_acc[which, p], l_acc[which, p], o_acc[which, p] = state

    def get(which, p):
        return m_acc[which, p], l_acc[which, p], o_acc[which, p]

    def scores_of(s, j_keys, j_queries, p):
        return dot(kb[s][j_keys, p], qbd[j_queries, p])

    def own_blocks(p):
        shape = (HALF, 2 * HALF)
        row = lax.broadcasted_iota(jnp.int32, shape, 0)
        col = lax.broadcasted_iota(jnp.int32, shape, 1)
        seen = row <= jnp.where(col < HALF, col, col - HALF)
        low = jnp.where(seen, scores_of(0, jl0, jl0, p), MASKED)
        cross = scores_of(0, jl0, 1 - jl0, p)
        high = jnp.where(seen, scores_of(0, 1 - jl0, 1 - jl0, p), MASKED)
        v_low, v_high = vb[0][jl0, p], vb[0][1 - jl0, p]
        return [(low, v_low)], [(cross, v_low), (high, v_high)]

    def choose(s):
        jls, lows = scalars(s)
        pick = (lows > low0).astype(jnp.int32)
        return s, jls, jls + pick - 2 * jls * pick, jl0 + pick - 2 * jl0 * pick, pick == 1

    def attend(offsets, also, last=False):
        chosen = [choose(s) for s in offsets]

        def body(p):
            if offsets:
                low_blocks, high_blocks = [], []
                m_low, l_low, o_low = get(0, p)
                m_high, l_high, o_high = get(1, p)
                low_tops, high_tops = [m_low], [m_high]
            else:
                low_blocks, high_blocks = own_blocks(p)
                low_tops, high_tops = [], []
            floating = []
            for s, jls, jk, jq, is_high in chosen:
                high_blocks.append((scores_of(s, jls, 1 - jl0, p), vb[s][jls, p]))
                scores = scores_of(s, jk, jq, p)
                floating.append((scores, vb[s][jk, p], is_high))
                top = highest(scores)
                high_tops.append(jnp.where(is_high, top, MASKED))
                low_tops.append(jnp.where(is_high, MASKED, top))
            low_tops += [highest(scores) for scores, _ in low_blocks]
            high_tops += [highest(scores) for scores, _ in high_blocks]
            low, high = low_tops[0], high_tops[0]
            for top in low_tops[1:]:
                low = jnp.maximum(low, top)
            for top in high_tops[1:]:
                high = jnp.maximum(high, top)
            for built in also:
                build_kv(*built, p)
            low_parts = [weigh(scores, low, values) for scores, values in low_blocks]
            high_parts = [weigh(scores, high, values) for scores, values in high_blocks]
            for scores, values, is_high in floating:
                total, out = weigh(scores, jnp.where(is_high, high, low), values)
                high_parts.append((jnp.where(is_high, total, 0.0), jnp.where(is_high, out, 0.0)))
                low_parts.append((jnp.where(is_high, 0.0, total), jnp.where(is_high, 0.0, out)))
            if offsets:
                fade = jnp.exp((m_low - low) * SCALE)
                low_parts.append((l_low * fade, o_low * fade))
                fade = jnp.exp((m_high - high) * SCALE)
                high_parts.append((l_high * fade, o_high * fade))
            l_low, o_low = (sum(parts[1:], parts[0]) for parts in zip(*low_parts))
            l_high, o_high = (sum(parts[1:], parts[0]) for parts in zip(*high_parts))

            def store():
                if not last:
                    put(0, p, (low, l_low, o_low))
                    put(1, p, (high, l_high, o_high))
                    return
                rows_low = turned_rows((o_low * (0.5 / l_low)).astype(BF16))
                rows_high = turned_rows((o_high * (0.5 / l_high)).astype(BF16))
                log_low = low * SCALE + jnp.log(l_low)
                log_high = high * SCALE + jnp.log(l_high)
                for j in range(2):
                    is_low = jl0 == j
                    rows = jnp.where(is_low, rows_low, rows_high)
                    out_ref[p, j * HALF : (j + 1) * HALF, :] = rows[:HALF]
                    out_ref[p + PAIRS, j * HALF : (j + 1) * HALF, :] = rows[HALF:]
                    logs[j, pl.ds(p, 1), :] = jnp.where(is_low, log_low, log_high)
                for head in (p, p + PAIRS):
                    write_out(head).start()

            return store

        loop(body, 2)

    def turned_rows(x):
        parts = [turn(x[:, i * DH : (i + 1) * DH]) for i in range(3)]
        return jnp.concatenate(parts, axis=0).astype(BF16)

    def write_out(head):
        return pltpu.make_async_copy(out_ref.at[head], out_hbm.at[head], out_sem.at[head])

    jl0, low0 = scalars(0)
    prep_a(0)
    prep_b(0, h)
    prep_aq()
    prep_q(h)
    build_all(kv(0, h), q(h))
    pass_on(kv_out, kv_on)
    wait_a(1)
    prep_a(1)
    prep_b(1, h)
    pass_on(q_out, q_on)
    wait_all(kv_on)
    send_b(0)
    prep_b(0, other)
    build_all(kv(0, other), kv(1, h))
    wait_a(2)
    wait_b(1)
    prep_b(1, other)
    wait_all(q_on)
    prep_q(other)
    build_all(kv(1, other), q(other))
    prep_a(2)
    prep_b(2, h)
    wait_b(2)
    prep_b(2, other)
    attend([], [(2, h), (2, other)])
    wait_a(3)
    prep_a(3)
    prep_b(3, h)
    attend([1], [(3, h)])
    wait_b(3)
    prep_b(3, other)
    build_all(kv(3, other))
    attend([2, 3], [], last=True)
    log0, log1 = logs[0], logs[1]
    log_ref[0:PAIRS] = jnp.where(first, log0, pltpu.roll(log1, HALF, 1))
    log_ref[PAIRS:] = jnp.where(first, pltpu.roll(log0, HALF, 1), log1)

    write_log = pltpu.make_async_copy(log_ref, log_hbm, out_sem.at[2 * PAIRS])
    write_log.start()

    for copy in kv_out + q_out + kv_on + q_on:
        copy.wait_send()
    for s in range(3):
        for copy in a_copies(s) + [b_copy(s)]:
            copy.wait_send()

    for head in range(2 * PAIRS):
        write_out(head).wait()
    write_log.wait()


def on_device(block_table, a_query, b_query, a_key, b_key, a_value, b_value):
    rows = 2 * HALF
    heads = 2 * PAIRS
    hbm = pl.BlockSpec(memory_space=pltpu.HBM)
    dma = pltpu.SemaphoreType.DMA
    return pl.pallas_call(
        kernel,
        out_shape=(
            jax.ShapeDtypeStruct((heads, rows, DH), BF16),
            jax.ShapeDtypeStruct((heads, rows), F32),
        ),
        in_specs=[pl.BlockSpec(memory_space=pltpu.SMEM)] + [hbm] * 6,
        out_specs=(hbm, hbm),
        scratch_shapes=[
            pltpu.VMEM((2, HALF, 2 * DH), BF16),
            pltpu.VMEM((2, HALF // 2, RQ * DH), BF16),
            pltpu.VMEM((heads, rows, DH), BF16),
            pltpu.VMEM((heads, rows), F32),
            pltpu.VMEM((4, 8, 128), jnp.int32),
            pltpu.SMEM((4, 8, 128), jnp.int32),
            pltpu.VMEM((RQ, heads, rows), BF16),
            pltpu.VMEM((2, HALF, RQ * DH), BF16),
            pltpu.VMEM((4, 2, 2, HALF, 2 * DH), BF16),
            pltpu.VMEM((4, 4, heads, rows), BF16),
            pltpu.VMEM((2, RQ * DH, rows), F32),
            pltpu.VMEM((2, RQ, PAIRS, rows), F32),
            pltpu.VMEM((2, PAIRS, 2 * DH, rows), BF16),
            pltpu.VMEM((4, 2, HALF, 2 * DH), F32),
            pltpu.VMEM((4, 2, 2 * DH, HALF), F32),
            pltpu.VMEM((4, 2, HALF, 4 * PAIRS), BF16),
            pltpu.VMEM((4, 2, 2, heads, HALF), F32),
            *[pltpu.VMEM((2, PAIRS, HALF, 2 * DH), BF16)] * 4,
            *[pltpu.VMEM((2, PAIRS, 2 * DH, HALF), BF16)] * 4,
            pltpu.VMEM((2, PAIRS, DH, rows), F32),
            pltpu.VMEM((2, PAIRS, 1, rows), F32),
            pltpu.VMEM((2, PAIRS, 1, rows), F32),
            pltpu.VMEM((2, PAIRS, rows), F32),
            pltpu.VMEM((2 * DH, 2 * DH), BF16),
            pltpu.VMEM((PAIRS, 4 * PAIRS, 4 * DH), BF16),
            dma((heads + 1,)),
            dma((6,)),
            dma((4,)),
            dma((8,)),
            dma((8,)),
            dma((3,)),
            dma((3,)),
            dma((3,)),
            dma((3,)),
            dma((3,)),
            dma((3,)),
            dma((3,)),
            dma((3,)),
        ],
        compiler_params=pltpu.CompilerParams(
            collective_id=0, has_side_effects=True, vmem_limit_bytes=60 * 1024 * 1024
        ),
    )(block_table, a_query, b_query, a_key, b_key, a_value, b_value)


def solution(mesh):
    in_specs = (
        P("blk", None),
        P(None, "head", "blk"),
        P(("blk", "head"), None),
        P(None, "head", "blk"),
        P(("blk", "head"), None),
        P(None, "head", "blk"),
        P(("blk", "head"), None),
    )
    out_specs = (P("head", "blk", None), P("head", "blk"))
    return jax.shard_map(
        on_device, mesh=mesh, in_specs=in_specs, out_specs=out_specs, check_vma=False
    )
```

```python
import math

import jax
import jax.numpy as jnp
from jax import lax
from jax.experimental import pallas as pl
from jax.experimental.pallas import tpu as pltpu
from jax.sharding import PartitionSpec as P

HALF = 192
DH = 128
PAIRS = 8
RQ = 6
MESH = pl.DeviceIdType.MESH
F32 = jnp.float32
BF16 = jnp.bfloat16
SCALE = 0.5 / math.sqrt(DH)
MASKED = -1e30


def kernel(
    bt_in, aq_in, bq_in, ak_in, bk_in, av_in, bv_in,
    out_hbm, log_hbm,
    relay_kv, relay_q, out_ref, log_ref, bt, bts, aq, bq, bkv, akv,
    bqt, a2q, qbd, bkf, bvt, akt, avj, kb0, kb1, kb2, kb3, vb0, vb1, vb2, vb3,
    o_acc, m_acc, l_acc, logs, ident, spread,
    out_sem, local_sem, bts_sem, ex_send, ex_recv, a_send, a_recv, f_send, f_recv, t_send, t_recv, b_send, b_recv,
):
    kb, vb = (kb0, kb1, kb2, kb3), (vb0, vb1, vb2, vb3)
    e = lax.axis_index("blk")
    h = lax.axis_index("head")
    places = lax.axis_size("blk")
    other = 1 - h
    core = lax.rem(e, 2)
    lane = lax.broadcasted_iota(jnp.int32, (1, 2 * HALF), 1)
    first = lane < HALF

    def at(blk, head):
        return {"blk": lax.rem(blk + places, places), "head": head}

    across = e + places // 2
    chip = lax.rem(e // 2, places // 4)
    leaves = jnp.logical_and(chip == places // 4 - 1, core == 1)
    enters = jnp.logical_and(chip == 0, core == 0)

    barrier = pltpu.get_barrier_semaphore()

    def greet(target):
        pl.semaphore_signal(barrier, inc=1, device_id=target, device_id_type=MESH)

    greet(at(across, h))
    greet(at(across, other))
    greet(at(e - 1, h))

    @pl.when(enters)
    def _():
        greet(at(e - 1, other))

    locals_ = [
        pltpu.make_async_copy(src, dst, local_sem.at[i])
        for i, (src, dst) in enumerate(
            [
                (bk_in, bkv.at[0, h, 0]),
                (bv_in, bkv.at[0, h, 1]),
                (ak_in, akv.at[0, pl.ds(0, 2)]),
                (av_in, akv.at[0, pl.ds(2, 2)]),
                (bq_in, bq.at[h]),
                (aq_in, aq),
            ]
        )
    ]
    for copy in locals_:
        copy.start()
    side = (2 * DH, 2 * DH)
    ident[...] = (
        lax.broadcasted_iota(jnp.int32, side, 0) == lax.broadcasted_iota(jnp.int32, side, 1)
    ).astype(F32).astype(BF16)
    side = (4 * PAIRS, 4 * DH)
    source = lax.broadcasted_iota(jnp.int32, side, 0)
    wanted = lax.broadcasted_iota(jnp.int32, side, 1) // DH * PAIRS
    for p in range(PAIRS):
        spread[p] = (source == wanted + p).astype(F32).astype(BF16)
    own0, own1 = bt_in[0, 0], bt_in[0, 1]
    tlane = lax.broadcasted_iota(jnp.int32, (8, 128), 1)
    bt[0] = jnp.where(tlane == 0, own0, own1)
    pltpu.make_async_copy(bt.at[0], bts.at[0], bts_sem.at[0]).start()

    pl.semaphore_wait(barrier, 3 + leaves.astype(jnp.int32))

    def remote(src, dst, send, recv, target):
        return pltpu.make_async_remote_copy(
            src_ref=src, dst_ref=dst, send_sem=send, recv_sem=recv, device_id=target, device_id_type=MESH
        )

    ahead = at(e + 1, h)
    half = jnp.where(leaves, h, other)
    ahead_b = at(e + 1, 1 - half)

    def a_copies(s):
        return [
            remote(bkv.at[s, h], bkv.at[s + 1, h], a_send.at[s], a_recv.at[s], ahead),
            remote(akv.at[s], akv.at[s + 1], f_send.at[s], f_recv.at[s], ahead),
            remote(bt.at[s], bt.at[s + 1], t_send.at[s], t_recv.at[s], ahead),
        ]

    def b_copy(s):
        return remote(bkv.at[s, half], bkv.at[s + 1, half], b_send.at[s], b_recv.at[s], ahead_b)

    def start(copies):
        for copy in copies:
            copy.start()

    def send_a(s):
        start(a_copies(s))

        @pl.when(leaves)
        def _():
            b_copy(s).start()

    def send_b(s):
        @pl.when(jnp.logical_not(leaves))
        def _():
            b_copy(s).start()

    def fetch(s):
        return pltpu.make_async_copy(bt.at[s], bts.at[s], bts_sem.at[s])

    def wait_a(s):
        for copy in a_copies(s - 1):
            copy.wait_recv()
        fetch(s).start()
        if s < 3:
            send_a(s)

    def wait_b(s):
        remote(
            bkv.at[s - 1, other], bkv.at[s, other], b_send.at[s - 1], b_recv.at[s - 1], ahead
        ).wait_recv()
        if s < 3:
            send_b(s)

    same, cross = at(across, h), at(across, other)
    half_rows = HALF // 2

    def q_part(half, i):
        return bq.at[half, pl.ds(i * half_rows, half_rows)]

    def out_copy(i, src, dst, target):
        return remote(src, dst, ex_send.at[i], ex_recv.at[i], target)

    kv_out = [
        out_copy(0, bkv.at[0, h, 0], relay_kv.at[0], same),
        out_copy(1, bkv.at[0, h, 1], relay_kv.at[1], cross),
    ]
    q_out = [
        out_copy(2, q_part(h, 0), relay_q.at[0], same),
        out_copy(3, q_part(h, 1), relay_q.at[1], cross),
    ]
    kv_on = [
        out_copy(4, relay_kv.at[0], bkv.at[0, h, 0], cross),
        out_copy(5, relay_kv.at[1], bkv.at[0, other, 1], same),
    ]
    q_on = [
        out_copy(6, relay_q.at[0], q_part(h, 0), cross),
        out_copy(7, relay_q.at[1], q_part(other, 1), same),
    ]

    def pass_on(arrived, onward):
        for before, after in zip(arrived, onward):
            before.wait_recv()
            after.start()

    def wait_all(copies):
        for copy in copies:
            copy.wait_recv()

    for copy in locals_[:4]:
        copy.wait()
    start(kv_out)
    send_a(0)
    locals_[4].wait()
    start(q_out)
    locals_[5].wait()

    def scalars(s):
        fetch(s).wait()
        b0, b1 = bts[s, 0, 0], bts[s, 0, 1]
        return (b0 > b1).astype(jnp.int32), jnp.minimum(b0, b1)

    def dot(x, y):
        return jnp.dot(x, y, preferred_element_type=F32)

    def turn(y):
        n = y.shape[1]
        return lax.dot_general(ident[:n, :n], y, (((1,), (1,)), ((), ())), preferred_element_type=F32)

    def prep_a(s):
        keys = akv[s, 0:2].reshape(4 * PAIRS, 2 * HALF)
        keys_t = jnp.concatenate([turn(keys[:, i * DH : (i + 1) * DH]) for i in range(3)], axis=0)
        akt[s, 0] = keys_t[:HALF].astype(BF16)
        akt[s, 1] = keys_t[HALF:].astype(BF16)
        values = akv[s, 2:4].astype(F32)
        avj[s, 0] = values[:, :, :HALF]
        avj[s, 1] = values[:, :, HALF:]

    def prep_b(s, j):
        bkf[s, j] = bkv[s, j, 0].astype(F32)
        bvt[s, j] = turn(bkv[s, j, 1])

    def prep_q(j):
        for i in range(RQ // 2):
            b = bq[j, :, i * 2 * DH : (i + 1) * 2 * DH]
            bqt[j, i * 2 * DH : (i + 1) * 2 * DH] = turn(jnp.concatenate([b, b], axis=0))

    def prep_aq():
        x = aq[...].astype(F32)
        low, high = x[:, :PAIRS], x[:, PAIRS:]
        wide = first[None]

        def turned(y):
            return pltpu.roll(y.reshape(RQ * PAIRS, 2 * HALF), HALF, 1).reshape(y.shape)

        a2q[0] = jnp.where(wide, low, turned(high))
        a2q[1] = jnp.where(wide, turned(low), high)

    def build_q(j, p):
        total = a2q[j, 0, pl.ds(p, 1), :] * bqt[j, 0:DH, :]
        for r in range(1, RQ):
            total += a2q[j, r, pl.ds(p, 1), :] * bqt[j, r * DH : (r + 1) * DH, :]
        total = total * (1.0 / RQ)
        qbd[j, p, 0:DH] = jnp.where(first, total, 0.0).astype(BF16)
        qbd[j, p, DH : 2 * DH] = jnp.where(first, 0.0, total).astype(BF16)

    def build_kv(s, j, p):
        wide = dot(akt[s, j], spread[p])
        b0, b1 = bkf[s, j, :, 0:DH], bkf[s, j, :, DH : 2 * DH]
        ka = wide[:, 0:DH] * b0 + wide[:, 2 * DH : 3 * DH] * b1
        kb_ = wide[:, DH : 2 * DH] * b0 + wide[:, 3 * DH :] * b1
        c0, c1 = bvt[s, j, 0:DH], bvt[s, j, DH : 2 * DH]
        va = avj[s, j, 0, pl.ds(p, 1), :] * c0 + avj[s, j, 1, pl.ds(p, 1), :] * c1
        vb_ = avj[s, j, 0, pl.ds(p + PAIRS, 1), :] * c0 + avj[s, j, 1, pl.ds(p + PAIRS, 1), :] * c1
        kb[s][j, p, :, 0:DH] = ka.astype(BF16)
        kb[s][j, p, :, DH : 2 * DH] = kb_.astype(BF16)
        vb[s][j, p, 0:DH] = va.astype(BF16)
        vb[s][j, p, DH : 2 * DH] = vb_.astype(BF16)

    middle = lax.broadcasted_iota(jnp.int32, (1, DH), 1) < HALF - DH

    def weigh(scores, top, values):
        weights = jnp.exp((scores - top) * SCALE)
        total = jnp.sum(weights, axis=0, keepdims=True)
        rounded = weights.astype(BF16)
        both = dot(values, rounded[:, : 2 * DH])
        last = dot(values[DH:], rounded[:, 2 * DH :])
        out = jnp.concatenate(
            [both[:DH, :DH], jnp.where(middle, both[:DH, DH:], both[DH:, DH:]), last], axis=1
        )
        return total, out

    def highest(scores):
        return jnp.max(scores, axis=0, keepdims=True)

    def loop(body, width):
        each = PAIRS // width

        def step(p, carry):
            done = [body(p + i * each) for i in range(width)]
            for store in done:
                if store is not None:
                    store()
            return carry

        lax.fori_loop(0, each, step, 0)

    def build_all(*builds):
        def body(p):
            for build in builds:
                build(p)

        loop(body, 4 if len(builds) == 1 else 2)

    def kv(s, j):
        return lambda p: build_kv(s, j, p)

    def q(j):
        return lambda p: build_q(j, p)

    def put(which, p, state):
        m_acc[which, p], l_acc[which, p], o_acc[which, p] = state

    def get(which, p):
        return m_acc[which, p], l_acc[which, p], o_acc[which, p]

    def scores_of(s, j_keys, j_queries, p):
        return dot(kb[s][j_keys, p], qbd[j_queries, p])

    def own_blocks(p):
        shape = (HALF, 2 * HALF)
        row = lax.broadcasted_iota(jnp.int32, shape, 0)
        col = lax.broadcasted_iota(jnp.int32, shape, 1)
        seen = row <= jnp.where(col < HALF, col, col - HALF)
        low = jnp.where(seen, scores_of(0, jl0, jl0, p), MASKED)
        cross = scores_of(0, jl0, 1 - jl0, p)
        high = jnp.where(seen, scores_of(0, 1 - jl0, 1 - jl0, p), MASKED)
        v_low, v_high = vb[0][jl0, p], vb[0][1 - jl0, p]
        return [(low, v_low)], [(cross, v_low), (high, v_high)]

    def choose(s):
        jls, lows = scalars(s)
        pick = (lows > low0).astype(jnp.int32)
        return s, jls, jls + pick - 2 * jls * pick, jl0 + pick - 2 * jl0 * pick, pick == 1

    def attend(offsets, also, last=False):
        chosen = [choose(s) for s in offsets]

        def body(p):
            if offsets:
                low_blocks, high_blocks = [], []
                m_low, l_low, o_low = get(0, p)
                m_high, l_high, o_high = get(1, p)
                low_tops, high_tops = [m_low], [m_high]
            else:
                low_blocks, high_blocks = own_blocks(p)
                low_tops, high_tops = [], []
            floating = []
            for s, jls, jk, jq, is_high in chosen:
                high_blocks.append((scores_of(s, jls, 1 - jl0, p), vb[s][jls, p]))
                scores = scores_of(s, jk, jq, p)
                floating.append((scores, vb[s][jk, p], is_high))
                top = highest(scores)
                high_tops.append(jnp.where(is_high, top, MASKED))
                low_tops.append(jnp.where(is_high, MASKED, top))
            low_tops += [highest(scores) for scores, _ in low_blocks]
            high_tops += [highest(scores) for scores, _ in high_blocks]
            low, high = low_tops[0], high_tops[0]
            for top in low_tops[1:]:
                low = jnp.maximum(low, top)
            for top in high_tops[1:]:
                high = jnp.maximum(high, top)
            for built in also:
                build_kv(*built, p)
            low_parts = [weigh(scores, low, values) for scores, values in low_blocks]
            high_parts = [weigh(scores, high, values) for scores, values in high_blocks]
            for scores, values, is_high in floating:
                total, out = weigh(scores, jnp.where(is_high, high, low), values)
                high_parts.append((jnp.where(is_high, total, 0.0), jnp.where(is_high, out, 0.0)))
                low_parts.append((jnp.where(is_high, 0.0, total), jnp.where(is_high, 0.0, out)))
            if offsets:
                fade = jnp.exp((m_low - low) * SCALE)
                low_parts.append((l_low * fade, o_low * fade))
                fade = jnp.exp((m_high - high) * SCALE)
                high_parts.append((l_high * fade, o_high * fade))
            l_low, o_low = (sum(parts[1:], parts[0]) for parts in zip(*low_parts))
            l_high, o_high = (sum(parts[1:], parts[0]) for parts in zip(*high_parts))

            def store():
                if not last:
                    put(0, p, (low, l_low, o_low))
                    put(1, p, (high, l_high, o_high))
                    return
                rows_low = turned_rows((o_low * (0.5 / l_low)).astype(BF16))
                rows_high = turned_rows((o_high * (0.5 / l_high)).astype(BF16))
                log_low = low * SCALE + jnp.log(l_low)
                log_high = high * SCALE + jnp.log(l_high)
                for j in range(2):
                    is_low = jl0 == j
                    rows = jnp.where(is_low, rows_low, rows_high)
                    out_ref[p, j * HALF : (j + 1) * HALF, :] = rows[:HALF]
                    out_ref[p + PAIRS, j * HALF : (j + 1) * HALF, :] = rows[HALF:]
                    logs[j, pl.ds(p, 1), :] = jnp.where(is_low, log_low, log_high)
                for head in (p, p + PAIRS):
                    write_out(head).start()

            return store

        loop(body, 2)

    def turned_rows(x):
        parts = [turn(x[:, i * DH : (i + 1) * DH]) for i in range(3)]
        return jnp.concatenate(parts, axis=0).astype(BF16)

    def write_out(head):
        return pltpu.make_async_copy(out_ref.at[head], out_hbm.at[head], out_sem.at[head])

    jl0, low0 = scalars(0)
    def on_core(which, wait, s):
        @pl.when(core == which)
        def _():
            wait(s)

    prep_a(0)
    prep_b(0, h)
    prep_aq()
    prep_q(h)
    build_all(kv(0, h), q(h))
    pass_on(kv_out, kv_on)
    on_core(1, wait_a, 1)
    pass_on(q_out, q_on)
    wait_all(kv_on)
    send_b(0)
    prep_b(0, other)
    wait_all(q_on)
    prep_q(other)
    build_all(kv(0, other), q(other))
    on_core(0, wait_a, 1)
    prep_a(1)
    prep_b(1, h)
    on_core(1, wait_a, 2)
    wait_b(1)
    prep_b(1, other)
    build_all(kv(1, h), kv(1, other))
    on_core(1, wait_b, 2)
    on_core(0, wait_a, 2)
    prep_a(2)
    prep_b(2, h)
    attend([], [(2, h)])
    on_core(0, wait_b, 2)
    prep_b(2, other)
    wait_a(3)
    prep_a(3)
    prep_b(3, h)
    attend([1], [(2, other), (3, h)])
    wait_b(3)
    prep_b(3, other)
    build_all(kv(3, other))
    attend([2, 3], [], last=True)
    log0, log1 = logs[0], logs[1]
    log_ref[0:PAIRS] = jnp.where(first, log0, pltpu.roll(log1, HALF, 1))
    log_ref[PAIRS:] = jnp.where(first, pltpu.roll(log0, HALF, 1), log1)

    write_log = pltpu.make_async_copy(log_ref, log_hbm, out_sem.at[2 * PAIRS])
    write_log.start()

    for copy in kv_out + q_out + kv_on + q_on:
        copy.wait_send()
    for s in range(3):
        for copy in a_copies(s) + [b_copy(s)]:
            copy.wait_send()

    for head in range(2 * PAIRS):
        write_out(head).wait()
    write_log.wait()


def on_device(block_table, a_query, b_query, a_key, b_key, a_value, b_value):
    rows = 2 * HALF
    heads = 2 * PAIRS
    hbm = pl.BlockSpec(memory_space=pltpu.HBM)
    dma = pltpu.SemaphoreType.DMA
    return pl.pallas_call(
        kernel,
        out_shape=(
            jax.ShapeDtypeStruct((heads, rows, DH), BF16),
            jax.ShapeDtypeStruct((heads, rows), F32),
        ),
        in_specs=[pl.BlockSpec(memory_space=pltpu.SMEM)] + [hbm] * 6,
        out_specs=(hbm, hbm),
        scratch_shapes=[
            pltpu.VMEM((2, HALF, 2 * DH), BF16),
            pltpu.VMEM((2, HALF // 2, RQ * DH), BF16),
            pltpu.VMEM((heads, rows, DH), BF16),
            pltpu.VMEM((heads, rows), F32),
            pltpu.VMEM((4, 8, 128), jnp.int32),
            pltpu.SMEM((4, 8, 128), jnp.int32),
            pltpu.VMEM((RQ, heads, rows), BF16),
            pltpu.VMEM((2, HALF, RQ * DH), BF16),
            pltpu.VMEM((4, 2, 2, HALF, 2 * DH), BF16),
            pltpu.VMEM((4, 4, heads, rows), BF16),
            pltpu.VMEM((2, RQ * DH, rows), F32),
            pltpu.VMEM((2, RQ, PAIRS, rows), F32),
            pltpu.VMEM((2, PAIRS, 2 * DH, rows), BF16),
            pltpu.VMEM((4, 2, HALF, 2 * DH), F32),
            pltpu.VMEM((4, 2, 2 * DH, HALF), F32),
            pltpu.VMEM((4, 2, HALF, 4 * PAIRS), BF16),
            pltpu.VMEM((4, 2, 2, heads, HALF), F32),
            *[pltpu.VMEM((2, PAIRS, HALF, 2 * DH), BF16)] * 4,
            *[pltpu.VMEM((2, PAIRS, 2 * DH, HALF), BF16)] * 4,
            pltpu.VMEM((2, PAIRS, DH, rows), F32),
            pltpu.VMEM((2, PAIRS, 1, rows), F32),
            pltpu.VMEM((2, PAIRS, 1, rows), F32),
            pltpu.VMEM((2, PAIRS, rows), F32),
            pltpu.VMEM((2 * DH, 2 * DH), BF16),
            pltpu.VMEM((PAIRS, 4 * PAIRS, 4 * DH), BF16),
            dma((heads + 1,)),
            dma((6,)),
            dma((4,)),
            dma((8,)),
            dma((8,)),
            dma((3,)),
            dma((3,)),
            dma((3,)),
            dma((3,)),
            dma((3,)),
            dma((3,)),
            dma((3,)),
            dma((3,)),
        ],
        compiler_params=pltpu.CompilerParams(
            collective_id=0, has_side_effects=True, vmem_limit_bytes=60 * 1024 * 1024
        ),
    )(block_table, a_query, b_query, a_key, b_key, a_value, b_value)


def solution(mesh):
    in_specs = (
        P("blk", None),
        P(None, "head", "blk"),
        P(("blk", "head"), None),
        P(None, "head", "blk"),
        P(("blk", "head"), None),
        P(None, "head", "blk"),
        P(("blk", "head"), None),
    )
    out_specs = (P("head", "blk", None), P("head", "blk"))
    return jax.shard_map(
        on_device, mesh=mesh, in_specs=in_specs, out_specs=out_specs, check_vma=False
    )
```
